512 devices in a mesh: rep: 8 (over z_hi, x), fsdp: 64 (over y, z_lo, core).
Axes of the slice: x: 4, y: 8, z: 8 (z_hi: 2, z_lo: 4; z = z_hi * 4 + z_lo), core: 2. Of those that a mesh axis runs over, the one named last changes fastest.
Arguments:
- activations: bfloat16 [8, 8192, 8192], P('rep', 'fsdp'), may hold values from -6 to 6
- cotangent: bfloat16 [8, 8192, 512], P('rep', 'fsdp'), may hold values from -6 to 6
- local_weight: bfloat16 [8, 8192, 512], P('rep', 'fsdp'), may hold values from -6 to 6
- norm_gain: float32 [8, 8192], P('rep', 'fsdp'), may hold values from 0.5 to 1.5
- global_weight: float32 [8192, 512], P('fsdp'), may hold values from -6 to 6
- momentum: float32 [8192, 512], P('fsdp'), may hold values from -4 to 4
- codes: bfloat16 [8, 8192, 512], P('rep', 'fsdp'), may hold values from -30 to 30, as said below
- exponents: int32 [8, 8192, 4], P('rep', 'fsdp'), may hold values from -7 to -3
Outputs:
- new_local: float32 [8, 8192, 512], P('rep', 'fsdp')
- new_gain: float32 [8, 8192], P('rep', 'fsdp')
- new_global: float32 [8192, 512], P('fsdp')
- new_momentum: float32 [8192, 512], P('fsdp')
The draws below stay inside these ranges and needn't reach their ends.
Inputs may be any that keep to these rules, and one draw needn't show every extreme that they name: `codes`: every entry is s (1 + m / 8) 2 ** k with s = 1 or -1, m in 0..7 and k in -3..4, a value of an 8-bit float with four exponent and three mantissa bits.
All inputs are finite; a program needn't handle non-finite values.
Results may differ from the reference program's by a relative error of at most 0.00038.
Values may be sent and summed in bfloat16 or wider, within the bound.
A program may use at most 64 MiB of HBM per device.

```python
import math
import jax
import jax.numpy as jnp
from jax import lax

D = 8192
KV = 512
BLOCK = 128
TOKENS = 8192
REPLICAS = 8
NB = 4
N_REP = 8


def draw_codes(key, part):
    key = jax.random.fold_in(key, 11)
    key_sign, key_mant, key_exp = jax.random.split(key, 3)
    shape = (REPLICAS, D, KV)
    signs = 2 * jax.random.randint(key_sign, shape, 0, 2) - 1
    mants = jax.random.randint(key_mant, shape, 0, 8)
    powers = jax.random.randint(key_exp, shape, -3, 5)
    values = signs.astype(jnp.float32) * (1.0 + mants.astype(jnp.float32) / 8.0) * jnp.exp2(powers.astype(jnp.float32))
    return values.astype(jnp.bfloat16)


def set_ends(entries, key, low, largest):
    place = [jax.random.randint(jax.random.fold_in(key, axis), (), 0, length) for axis, length in enumerate(entries.shape)]
    widest = entries.shape.index(max(entries.shape))
    next_to = place[:widest] + [(place[widest] + 1) % entries.shape[widest]] + place[widest + 1:]
    return entries.at[tuple(place)].set(low).at[tuple(next_to)].set(largest)


def block_levels(own_key, extent, cuts, smallest, top_value):
    loudness, own = 1.0, jax.random.fold_in(own_key, 6)
    for axis_at, blocks in cuts:
        heights = jnp.exp(jax.random.uniform(jax.random.fold_in(own, axis_at), (blocks,), jnp.float32, smallest / len(cuts), top_value / len(cuts)))
        loudness = loudness * jnp.repeat(heights, extent[axis_at] // blocks).reshape([-1 if axis == axis_at else 1 for axis in range(len(extent))])
    return loudness


def centred(stream_key, shape, spread, reach, cuts=(), kind=jnp.bfloat16):
    drawn = jax.random.normal(stream_key, shape, jnp.float32) * spread
    if len(cuts) > 0:
        drawn = block_levels(stream_key, shape, cuts, -0.22, 0.18) * drawn
    return jnp.clip(drawn, min=-reach, max=reach).astype(kind)


def setup_inputs(seed: int = 0) -> dict:
    keys = jax.random.split(jax.random.key(seed), 9)
    return {
        "activations": centred(keys[0], (REPLICAS, TOKENS, D), 1.0, 6.0, ((0, 8), (1, 64))),
        "cotangent": centred(keys[1], (REPLICAS, TOKENS, KV), 1.0, 6.0, ((0, 8), (1, 64))),
        "local_weight": centred(keys[2], (REPLICAS, D, KV), 1.0, 6.0, ((0, 8), (1, 64))),
        "norm_gain": jnp.clip(1.0 + 0.1 * jax.random.normal(keys[3], (REPLICAS, D), jnp.float32), 0.5, 1.5),
        "global_weight": centred(keys[4], (D, KV), 1.0, 6.0, ((0, 64),), jnp.float32),
        "momentum": centred(keys[5], (D, KV), 0.3, 4.0, ((0, 64),), jnp.float32),
        "codes": draw_codes(jax.random.fold_in(keys[8], 71), 0),
        "exponents": set_ends(jax.random.randint(keys[7], (REPLICAS, D, NB), -7, -2), jax.random.fold_in(keys[7], 1), -7, (-2) - 1).astype(jnp.int32),
    }


def inner_step(pieces):
    hidden, grad_keys, weight, gain = pieces
    values = hidden.astype(jnp.float32)
    normed = (values * lax.rsqrt(lax.optimization_barrier(jnp.mean(values * values, axis=-1, keepdims=True)) + 1e-05)).astype(jnp.bfloat16)
    product = lax.dot_general(normed, grad_keys, (((0,), (0,)), ((), ())), preferred_element_type=jnp.float32)
    weight_grad = gain[:, None] * product / math.sqrt(D)
    scaled_grad = lax.dot_general(grad_keys, weight, (((1,), (1,)), ((), ())), preferred_element_type=jnp.float32) / math.sqrt(D)
    gain_grad = lax.optimization_barrier(jnp.sum(scaled_grad * normed.astype(jnp.float32), axis=0))
    return (weight.astype(jnp.float32) - 0.2 * weight_grad, gain - 0.005 * gain_grad)

def reference(activations, cotangent, local_weight, norm_gain, global_weight, momentum, codes, exponents):
    scales = jnp.exp2(exponents.astype(jnp.float32))
    decoded = codes.astype(jnp.float32).reshape(REPLICAS, D, NB, BLOCK) * scales[..., None]
    average = lax.optimization_barrier(jnp.sum(decoded.reshape(REPLICAS, D, KV), axis=0)) / N_REP
    new_momentum = 0.9 * momentum + average
    new_global = global_weight - 0.7 * (average + 0.9 * new_momentum)
    stepped, new_gain = lax.map(inner_step, (activations, cotangent, local_weight, norm_gain))
    new_local = 0.5 * stepped + 0.5 * new_global[None]
    return (new_local, new_gain, new_global, new_momentum)
```

```python
import functools
import math

import jax
import jax.numpy as jnp
from jax import lax
from jax.experimental import pallas as pl
from jax.experimental.pallas import tpu as pltpu
from jax.sharding import PartitionSpec as P

MESH = pl.DeviceIdType.MESH
YS, ZS, XS = 8, 4, 4
F32, BF16 = jnp.float32, jnp.bfloat16


def flip(value, mask):
    low, high = lax.rem(value, 2), value // 2
    if mask & 1:
        low = 1 - low
    if mask & 2:
        high = 1 - high
    return high * 2 + low


def column(row, eye):
    return jnp.sum(jnp.where(eye, row, 0.0), axis=1, keepdims=True)


def product(lhs, rhs):
    return lax.dot_general(lhs, rhs, (((0,), (0,)), ((), ())), preferred_element_type=F32)


def kernel(
    act_hbm, cot_hbm, weight_hbm, gain_hbm, global_hbm, momentum_hbm, codes_hbm, exps_hbm,
    local_out, gain_out, global_out, momentum_out,
    act, normed, recv, cots, weight, gain, outer, mom, codes, exps,
    part_sib, part_own, from_sib, from_z, decoded, x_in, x_sum, h_in, total,
    in_sem, cot_s, cot_r, a2a_s, a2a_r, sib_s, sib_r, z_s, z_r, x1_s, x1_r, h_s, h_r, x2_s, x2_r,
):
    rep, pos = lax.axis_index("rep"), lax.axis_index("fsdp")
    zh, x = rep // XS, lax.rem(rep, XS)
    y, z, core = pos // (2 * ZS), lax.rem(pos // 2, ZS), lax.rem(pos, 2)
    width = act.shape[1]

    def at(yy=None, zz=None, cc=None, xx=None, hh=None):
        yy = y if yy is None else yy
        zz = z if zz is None else zz
        cc = core if cc is None else cc
        xx = x if xx is None else xx
        hh = zh if hh is None else hh
        return (hh * XS + xx, (yy * ZS + zz) * 2 + cc)

    def y_off(d):
        return at(yy=lax.rem(y + d, YS))

    def x_off(d):
        return at(xx=lax.rem(x + d, XS))

    def send(src, dst, ssem, rsem, device):
        return pltpu.make_async_remote_copy(
            src_ref=src, dst_ref=dst, send_sem=ssem, recv_sem=rsem, device_id=device, device_id_type=MESH
        )

    sibling = at(cc=1 - core)
    other = at(hh=1 - zh)

    loads = [
        pltpu.make_async_copy(cot_hbm.at[0], cots.at[0], in_sem.at[0]),
        pltpu.make_async_copy(codes_hbm.at[0], codes, in_sem.at[1]),
        pltpu.make_async_copy(exps_hbm, exps, in_sem.at[2]),
        pltpu.make_async_copy(act_hbm.at[0], act, in_sem.at[3]),
        pltpu.make_async_copy(weight_hbm.at[0], weight, in_sem.at[4]),
        pltpu.make_async_copy(gain_hbm, gain, in_sem.at[5]),
        pltpu.make_async_copy(global_hbm, outer, in_sem.at[6]),
        pltpu.make_async_copy(momentum_hbm, mom, in_sem.at[7]),
    ]
    for load in loads:
        load.start()

    barrier = pltpu.get_barrier_semaphore()
    peers = [y_off(d) for d in range(1, YS)] + [at(zz=flip(z, q)) for q in (1, 2, 3)]
    peers += [sibling, other] + [x_off(d) for d in range(1, XS)]
    for peer in peers:
        pl.semaphore_signal(barrier, inc=1, device_id=peer, device_id_type=MESH)

    eye = lax.broadcasted_iota(jnp.int32, (128, 128), 0) == lax.broadcasted_iota(
        jnp.int32, (128, 128), 1
    )
    loads[1].wait()
    loads[2].wait()
    scales = jnp.exp2(exps[...].astype(F32))
    for b in range(4):
        cols = slice(b * 128, (b + 1) * 128)
        scale = column(scales[b : b + 1, :], eye)
        decoded[:, cols] = (codes[:, cols].astype(F32) * scale).astype(BF16)

    pl.semaphore_wait(barrier, len(peers))

    up, down = y_off(1), y_off(YS - 1)
    loads[0].wait()
    hops_up = [send(cots.at[i], cots.at[i + 1], cot_s.at[i], cot_r.at[i], up) for i in range(3)]
    hops_up.append(send(cots.at[3, 0:64], cots.at[4, 0:64], cot_s.at[3], cot_r.at[3], up))
    hops_down = [
        send(cots.at[(8 - i) % 8], cots.at[7 - i], cot_s.at[4 + i], cot_r.at[4 + i], down)
        for i in range(3)
    ]
    hops_down.append(send(cots.at[5, 64:128], cots.at[4, 64:128], cot_s.at[7], cot_r.at[7], down))
    hops_up[0].start()
    hops_down[0].start()

    x_parts = []
    for d in range(1, XS):
        rows = pl.ds(pl.multiple_of(lax.rem(x + d, XS) * 32, 32), 32)
        x_parts.append(send(decoded.at[rows], x_in.at[d - 1], x1_s.at[d - 1], x1_r.at[d - 1], x_off(d)))
    for part in x_parts:
        part.start()

    loads[3].wait()

    @pl.loop(0, 8)
    def _(group):
        rows = pl.ds(pl.multiple_of(group * 16, 16), 16)
        squares = jnp.zeros((16, 256), F32)
        for b in range(32):
            values = act[rows, b * 256 : (b + 1) * 256].astype(F32)
            squares += values * values
        mean = jnp.sum(squares, axis=1, keepdims=True) / width
        scale = lax.rsqrt(mean + 1e-05)
        for b in range(32):
            values = act[rows, b * 256 : (b + 1) * 256].astype(F32)
            normed[b, rows, :] = (values * scale).astype(BF16)

    def push(k):
        zz = flip(z, 3 - k)
        for d in range(1, YS):
            yy = lax.rem(y + d, YS)
            send(normed.at[yy * ZS + zz], recv.at[k, d], a2a_s.at[k], a2a_r.at[k], at(yy=yy)).start()
        recv[k, 0] = normed[y * ZS + zz]

    def multiply(k):
        seven = pltpu.make_async_copy(recv.at[k, 1:8], recv.at[k, 1:8], a2a_r.at[k])
        seven.wait()
        rhs = cots[...].reshape(1024, 512)

        def part(c):
            cols = pl.ds(pl.multiple_of(c * 128, 128), 128)
            return product(recv[k, :, :, cols].reshape(1024, 128), rhs)

        part_sib[k] = part(1 - core)
        send(part_sib.at[k], from_sib.at[k], sib_s.at[k], sib_r.at[k], sibling).start()
        part_own[k] = part(core)

    def sib_copy(k):
        return send(part_sib.at[k], from_sib.at[k], sib_s.at[k], sib_r.at[k], sibling)

    def z_copy(k):
        return send(part_own.at[k], from_z.at[k], z_s.at[k], z_r.at[k], at(zz=flip(z, 3 - k)))

    def scatter(k):
        sib_copy(k).wait_recv()
        part_own[k] = part_own[k] + from_sib[k]
        z_copy(k).start()

    push(0)
    hops_up[0].wait_recv()
    hops_down[0].wait_recv()
    hops_up[1].start()
    hops_down[1].start()
    push(1)

    for part in x_parts:
        part.wait_recv()
    mine = pl.ds(pl.multiple_of(x * 32, 32), 32)
    x_sum[...] = (
        decoded[mine, :].astype(F32) + x_in[0].astype(F32) + x_in[1].astype(F32) + x_in[2].astype(F32)
    )
    h_copy = send(x_sum, h_in, h_s.at[0], h_r.at[0], other)
    h_copy.start()

    hops_up[1].wait_recv()
    hops_down[1].wait_recv()
    hops_up[2].start()
    hops_down[2].start()

    h_copy.wait_recv()
    total[mine, :] = x_sum[...] + h_in[...]
    totals = [
        send(total.at[mine], total.at[mine], x2_s.at[d - 1], x2_r.at[d - 1], x_off(d))
        for d in range(1, XS)
    ]
    for copy in totals:
        copy.start()

    hops_up[2].wait_recv()
    hops_down[2].wait_recv()
    hops_up[3].start()
    hops_down[3].start()
    push(2)
    hops_up[3].wait_recv()
    hops_down[3].wait_recv()

    multiply(0)
    push(3)
    scatter(0)
    multiply(1)
    scatter(1)

    for copy in totals:
        copy.wait_recv()
    for load in loads[4:]:
        load.wait()
    average = total[...] / 8.0
    momentum = 0.9 * mom[...] + average
    momentum_out[...] = momentum
    outer_new = outer[...] - 0.7 * (average + 0.9 * momentum)
    global_out[...] = outer_new

    multiply(2)
    scatter(2)
    multiply(3)
    for k in range(3):
        z_copy(k).wait_recv()
    sib_copy(3).wait_recv()
    summed = part_own[3] + from_sib[3] + from_z[0] + from_z[1] + from_z[2]

    root = math.sqrt(width)
    held = weight[...].astype(F32)
    gain_grad = jnp.sum(held * summed, axis=1, keepdims=True) / root
    gain_row = jnp.sum(jnp.where(eye, gain_grad, 0.0), axis=0, keepdims=True)
    gain_out[...] = gain[...] - 0.005 * gain_row
    weight_grad = column(gain[...], eye) * summed / root
    local_out[0] = 0.5 * (held - 0.2 * weight_grad) + 0.5 * global_out[...]

    for copy in hops_up + hops_down + x_parts + [h_copy] + totals:
        copy.wait_send()
    for k in range(4):
        pltpu.make_async_copy(normed.at[0:7], normed.at[0:7], a2a_s.at[k]).wait()
        sib_copy(k).wait_send()
    for k in range(3):
        z_copy(k).wait_send()


def shards(
    activations, cotangent, local_weight, norm_gain, global_weight, momentum, codes, exponents
):
    rows, width = global_weight.shape
    any_spec = pl.BlockSpec(memory_space=pl.ANY)
    vmem_spec = pl.BlockSpec(memory_space=pltpu.VMEM)
    sem = pltpu.SemaphoreType.DMA
    out_shape = (
        jax.ShapeDtypeStruct((1, rows, width), F32),
        jax.ShapeDtypeStruct((1, rows), F32),
        jax.ShapeDtypeStruct((rows, width), F32),
        jax.ShapeDtypeStruct((rows, width), F32),
    )
    return pl.pallas_call(
        kernel,
        out_shape=out_shape,
        in_specs=[any_spec] * 8,
        out_specs=(vmem_spec,) * 4,
        scratch_shapes=[
            pltpu.VMEM((128, 8192), BF16),
            pltpu.VMEM((32, 128, 256), BF16),
            pltpu.VMEM((4, 8, 128, 256), BF16),
            pltpu.VMEM((8, 128, 512), BF16),
            pltpu.VMEM((128, 512), BF16),
            pltpu.VMEM((1, 128), F32),
            pltpu.VMEM((128, 512), F32),
            pltpu.VMEM((128, 512), F32),
            pltpu.VMEM((128, 512), BF16),
            pltpu.VMEM((4, 128), jnp.int32),
            pltpu.VMEM((4, 128, 512), F32),
            pltpu.VMEM((4, 128, 512), F32),
            pltpu.VMEM((4, 128, 512), F32),
            pltpu.VMEM((3, 128, 512), F32),
            pltpu.VMEM((128, 512), BF16),
            pltpu.VMEM((3, 32, 512), BF16),
            pltpu.VMEM((32, 512), F32),
            pltpu.VMEM((32, 512), F32),
            pltpu.VMEM((128, 512), F32),
            sem((8,)),
            sem((8,)),
            sem((8,)),
            sem((4,)),
            sem((4,)),
            sem((4,)),
            sem((4,)),
            sem((3,)),
            sem((3,)),
            sem((3,)),
            sem((3,)),
            sem((1,)),
            sem((1,)),
            sem((3,)),
            sem((3,)),
        ],
        compiler_params=pltpu.CompilerParams(
            collective_id=0, has_side_effects=True, vmem_limit_bytes=40 << 20
        ),
        name="sync_and_step",
    )(
        activations, cotangent, local_weight, norm_gain, global_weight, momentum, codes,
        jnp.transpose(exponents[0]),
    )


def solution(mesh):
    placed = (
        P("rep", "fsdp", None),
        P("rep", "fsdp", None),
        P("rep", "fsdp", None),
        P("rep", "fsdp"),
        P("fsdp", None),
        P("fsdp", None),
        P("rep", "fsdp", None),
        P("rep", "fsdp", None),
    )
    return jax.shard_map(
        shards,
        mesh=mesh,
        in_specs=placed,
        out_specs=(P("rep", "fsdp", None), P("rep", "fsdp"), P("fsdp", None), P("fsdp", None)),
        check_vma=False,
    )
```

```python
import functools
import math

import jax
import jax.numpy as jnp
from jax import lax
from jax.experimental import pallas as pl
from jax.experimental.pallas import tpu as pltpu
from jax.sharding import PartitionSpec as P

MESH = pl.DeviceIdType.MESH
YS, ZS, XS = 8, 4, 4
F32, BF16 = jnp.float32, jnp.bfloat16


def flip(value, mask):
    low, high = lax.rem(value, 2), value // 2
    if mask & 1:
        low = 1 - low
    if mask & 2:
        high = 1 - high
    return high * 2 + low


def column(row, eye):
    return jnp.sum(jnp.where(eye, row, 0.0), axis=1, keepdims=True)


def product(lhs, rhs):
    return lax.dot_general(lhs, rhs, (((0,), (0,)), ((), ())), preferred_element_type=F32)


def kernel(
    act_hbm, cot_hbm, codes_hbm, exps_hbm, summed_hbm, total_hbm,
    act, cot, normed_y, normed_z, recv_y, recv_z, cots_y, cots_z, codes, exps,
    part, from_z, up_half, down_half, ups, downs, decoded, x_in, x_sum, h_in, total,
    in_sem, out_sem, cy_s, cy_r, cz_s, cz_r, ay_s, ay_r, az_s, az_r, own_s,
    z_s, z_r, up_s, up_r, down_s, down_r, x1_s, x1_r, h_s, h_r, x2_s, x2_r,
):
    rep, pos = lax.axis_index("rep"), lax.axis_index("fsdp")
    zh, x = rep // XS, lax.rem(rep, XS)
    y, z, core = pos // (2 * ZS), lax.rem(pos // 2, ZS), lax.rem(pos, 2)
    width = act.shape[1]

    def at(yy=None, zz=None, cc=None, xx=None, hh=None):
        yy = y if yy is None else yy
        zz = z if zz is None else zz
        cc = core if cc is None else cc
        xx = x if xx is None else xx
        hh = zh if hh is None else hh
        return (hh * XS + xx, (yy * ZS + zz) * 2 + cc)

    def y_off(d):
        return lax.rem(y + d, YS)

    def x_off(d):
        return at(xx=lax.rem(x + d, XS))

    def send(src, dst, ssem, rsem, device):
        return pltpu.make_async_remote_copy(
            src_ref=src, dst_ref=dst, send_sem=ssem, recv_sem=rsem, device_id=device, device_id_type=MESH
        )

    def greet(device):
        pl.semaphore_signal(barrier, inc=1, device_id=device, device_id_type=MESH)

    other = at(hh=1 - zh)

    loads = [
        pltpu.make_async_copy(cot_hbm.at[0], cot, in_sem.at[0]),
        pltpu.make_async_copy(codes_hbm.at[0], codes, in_sem.at[1]),
        pltpu.make_async_copy(exps_hbm, exps, in_sem.at[2]),
        pltpu.make_async_copy(act_hbm.at[0], act, in_sem.at[3]),
    ]
    for load in loads:
        load.start()

    barrier = pltpu.get_barrier_semaphore()
    for device in [at(cc=1 - core), other] + [x_off(d) for d in range(1, XS)]:
        greet(device)
    for q in (1, 2, 3):
        greet(at(zz=flip(z, q)))

    @pl.when(core == 0)
    def _():
        for d in range(1, YS):
            for c in range(2):
                greet(at(yy=y_off(d), cc=c))

    @pl.when(core == 1)
    def _():
        for q in (1, 2, 3):
            greet(at(zz=flip(z, q), cc=0))
        greet(at(yy=y_off(1)))
        greet(at(yy=y_off(7)))

    eye = lax.broadcasted_iota(jnp.int32, (128, 128), 0) == lax.broadcasted_iota(
        jnp.int32, (128, 128), 1
    )
    loads[1].wait()
    loads[2].wait()
    scales = jnp.exp2(exps[...].astype(F32))
    for b in range(4):
        cols = slice(b * 128, (b + 1) * 128)
        scale = column(scales[b : b + 1, :], eye)
        decoded[:, cols] = (codes[:, cols].astype(F32) * scale).astype(BF16)

    pl.semaphore_wait(barrier, 15 + jnp.where(core == 0, 3, 2))

    loads[0].wait()
    first = [
        send(cot, cots_y.at[1, core], cy_s.at[0], cy_r.at[0], at(yy=y_off(1), cc=0)),
        send(cot, cots_y.at[7, core], cy_s.at[4], cy_r.at[4], at(yy=y_off(7), cc=0)),
    ]
    for copy in first:
        copy.start()

    def first_right():
        return send(cot, cots_z.at[z, core], cz_s.at[0], cz_r.at[0], at(zz=z + 1, cc=1))

    def first_left():
        return send(cot, cots_z.at[z, core], cz_s.at[3], cz_r.at[3], at(zz=z - 1, cc=1))

    @pl.when(z < ZS - 1)
    def _():
        first_right().start()

    @pl.when(z > 0)
    def _():
        first_left().start()

    x_parts = []
    for d in range(1, XS):
        rows = pl.ds(pl.multiple_of(lax.rem(x + d, XS) * 32, 32), 32)
        x_parts.append(send(decoded.at[rows], x_in.at[d - 1], x1_s.at[d - 1], x1_r.at[d - 1], x_off(d)))
    for copy in x_parts:
        copy.start()

    def across_0():
        return send(cot, cots_z.at[z, 0], own_s.at[0], cz_r.at[6], at(cc=1))

    def across_1():
        return send(cot, cots_y.at[0, 1], own_s.at[0], cy_r.at[8], at(cc=0))

    @pl.when(core == 0)
    def _():
        across_0().start()
        cots_y[0, 0] = cot[...]

    @pl.when(core == 1)
    def _():
        across_1().start()
        cots_z[z, 1] = cot[...]

    loads[3].wait()

    @pl.loop(0, 8)
    def _(group):
        rows = pl.ds(pl.multiple_of(group * 16, 16), 16)
        squares = jnp.zeros((16, 256), F32)
        for b in range(32):
            values = act[rows, b * 256 : (b + 1) * 256].astype(F32)
            squares += values * values
        mean = jnp.sum(squares, axis=1, keepdims=True) / width
        scale = lax.rsqrt(mean + 1e-05)
        for b in range(32):
            values = act[rows, b * 256 : (b + 1) * 256].astype(F32)
            result = (values * scale).astype(BF16)
            normed_y[b, rows, :] = result[:, :128]
            normed_z[b // ZS + (b % ZS) * YS, rows, :] = result[:, 128:]

    def push_y(k):
        zz = flip(z, 3 - k)
        for d in (4, 3, 5, 2, 6, 1, 7):
            yy = y_off(d)
            send(
                normed_y.at[yy * ZS + zz], recv_y.at[k, 2 * d + core], ay_s.at[k], ay_r.at[k], at(yy=yy, cc=0)
            ).start()

        @pl.when(core == 0)
        def _():
            recv_y[k, 0] = normed_y[y * ZS + zz]

        @pl.when(core == 1)
        def _():
            own_y(k).start()

    def own_y(k):
        zz = flip(z, 3 - k)
        return send(normed_y.at[y * ZS + zz], recv_y.at[k, 1], own_s.at[1 + k], ay_r.at[k], at(cc=0))

    offsets = (4, 3, 5, 2, 6, 1, 7, 0)
    groups = ((0,), (1, 2), (3, 4), (5, 6), (7,))

    def push_z(g):
        for i in groups[g]:
            yy = y_off(offsets[i])
            for q in (3, 2, 1):
                zz = flip(z, q)
                send(
                    normed_z.at[zz * YS + yy], recv_z.at[i, z * 2 + core],
                    az_s.at[g], az_r.at[g], at(zz=zz, cc=1),
                ).start()

        @pl.when(core == 0)
        def _():
            for i in groups[g]:
                own_z(g, i).start()

        @pl.when(core == 1)
        def _():
            for i in groups[g]:
                recv_z[i, z * 2 + 1] = normed_z[z * YS + y_off(offsets[i])]

    def own_z(g, i):
        return send(
            normed_z.at[z * YS + y_off(offsets[i])], recv_z.at[i, z * 2],
            own_s.at[1 + i], az_r.at[g], at(cc=1),
        )

    def z_copy(k):
        return send(part.at[k], from_z.at[k], z_s.at[k], z_r.at[k], at(zz=flip(z, 3 - k)))

    def multiply_y(k):
        pltpu.make_async_copy(recv_y.at[k, 1:16], recv_y.at[k, 1:16], ay_r.at[k]).wait()
        part[k] = product(recv_y[k].reshape(2048, 128), cots_y[...].reshape(2048, 512))
        if k < 3:
            z_copy(k).start()

    def multiply_z(g):
        i, n = groups[g][0], len(groups[g])
        pltpu.make_async_copy(recv_z.at[i : i + n, 0:7], recv_z.at[i : i + n, 0:7], az_r.at[g]).wait()
        for i in groups[g]:
            part[i] = product(recv_z[i].reshape(1024, 128), cots_z[...].reshape(1024, 512))

    def up_copy(s):
        src = part.at[0, :, 0:256] if s == 0 else part.at[2 * s - 1]
        dst = up_half if s == 0 else ups.at[s - 1]
        return send(src, dst, up_s.at[s], up_r.at[s], at(yy=y_off(1)))

    def down_copy(s):
        src = part.at[0, :, 256:512] if s == 0 else part.at[2 * s]
        dst = down_half if s == 0 else downs.at[s - 1]
        return send(src, dst, down_s.at[s], down_r.at[s], at(yy=y_off(7)))

    def chain(s):
        if s > 0:
            up_copy(s - 1).wait_recv()
        if s == 1:
            part[1, :, 0:256] = part[1, :, 0:256] + up_half[...]
        elif s > 1:
            part[2 * s - 1] = part[2 * s - 1] + ups[s - 2]
        up_copy(s).start()
        if s > 0:
            down_copy(s - 1).wait_recv()
        if s == 1:
            part[2, :, 256:512] = part[2, :, 256:512] + down_half[...]
        elif s > 1:
            part[2 * s] = part[2 * s] + downs[s - 2]
        down_copy(s).start()

    def ring_up(i):
        if i < 3:
            return send(cots_y.at[i], cots_y.at[i + 1], cy_s.at[i], cy_r.at[i], at(yy=y_off(1)))
        return send(cots_y.at[3, 0], cots_y.at[4, 0], cy_s.at[3], cy_r.at[3], at(yy=y_off(1)))

    def ring_down(i):
        if i < 3:
            return send(cots_y.at[8 - i], cots_y.at[7 - i], cy_s.at[4 + i], cy_r.at[4 + i], at(yy=y_off(7)))
        return send(cots_y.at[5, 1], cots_y.at[4, 1], cy_s.at[7], cy_r.at[7], at(yy=y_off(7)))

    def ring_wait(i):
        if i == 0:
            pltpu.make_async_copy(cots_y.at[1], cots_y.at[1], cy_r.at[0]).wait()
            pltpu.make_async_copy(cots_y.at[7], cots_y.at[7], cy_r.at[4]).wait()
        else:
            ring_up(i).wait_recv()
            ring_down(i).wait_recv()

    def ring_go(i):
        ring_up(i).start()
        ring_down(i).start()

    def right(h):
        return send(cots_z.at[z - h], cots_z.at[z - h], cz_s.at[h], cz_r.at[h], at(zz=z + 1))

    def left(h):
        return send(cots_z.at[z + h], cots_z.at[z + h], cz_s.at[3 + h], cz_r.at[3 + h], at(zz=z - 1))

    def line_wait(h):
        @pl.when(z >= h)
        def _():
            pltpu.make_async_copy(cots_z.at[0], cots_z.at[0], cz_r.at[h - 1]).wait()

        @pl.when(z < ZS - h)
        def _():
            pltpu.make_async_copy(cots_z.at[0], cots_z.at[0], cz_r.at[2 + h]).wait()

        if h < 3:

            @pl.when((z >= h) & (z < ZS - 1))
            def _():
                right(h).start()

            @pl.when((z < ZS - h) & (z > 0))
            def _():
                left(h).start()

    mine = pl.ds(pl.multiple_of(x * 32, 32), 32)
    h_copy = send(x_sum, h_in, h_s.at[0], h_r.at[0], other)
    totals = [
        send(total.at[mine], total.at[mine], x2_s.at[d - 1], x2_r.at[d - 1], x_off(d))
        for d in range(1, XS)
    ]

    def spread_total():
        h_copy.wait_recv()
        total[mine, :] = x_sum[...] + h_in[...]
        for copy in totals:
            copy.start()

    total_copy = pltpu.make_async_copy(total, total_hbm, out_sem.at[0])

    def write_total():
        for copy in totals:
            copy.wait_recv()
        total_copy.start()

    push_z(0)
    push_y(0)
    for copy in x_parts:
        copy.wait_recv()
    x_sum[...] = (
        decoded[mine, :].astype(F32) + x_in[0].astype(F32) + x_in[1].astype(F32) + x_in[2].astype(F32)
    )
    h_copy.start()

    @pl.when(core == 0)
    def _():
        push_z(1)
        ring_wait(0)
        ring_go(1)
        push_z(2)
        ring_wait(1)
        ring_go(2)
        push_y(1)
        push_z(3)
        ring_wait(2)
        ring_go(3)
        push_z(4)
        push_y(2)
        push_y(3)
        spread_total()
        across_1().wait_recv()
        ring_wait(3)
        multiply_y(0)
        multiply_y(1)
        multiply_y(2)
        write_total()
        multiply_y(3)
        for k in range(3):
            z_copy(k).wait_recv()
        part[3] = part[3] + from_z[0] + from_z[1] + from_z[2]
        result = pltpu.make_async_copy(part.at[3], summed_hbm, out_sem.at[1])
        result.start()
        result.wait()

    @pl.when(core == 1)
    def _():
        line_wait(1)
        push_z(1)
        line_wait(2)
        push_y(1)
        push_z(2)
        push_z(3)
        line_wait(3)
        push_y(2)
        push_z(4)
        across_0().wait_recv()
        multiply_z(0)
        chain(0)
        push_y(3)
        multiply_z(1)
        chain(1)
        spread_total()
        multiply_z(2)
        chain(2)
        write_total()
        multiply_z(3)
        chain(3)
        multiply_z(4)
        up_copy(3).wait_recv()
        down_copy(3).wait_recv()
        part[7] = part[7] + ups[2] + downs[2]
        result = pltpu.make_async_copy(part.at[7], summed_hbm, out_sem.at[1])
        result.start()
        result.wait()

    total_copy.wait()
    for copy in first + x_parts + [h_copy] + totals:
        copy.wait_send()
    for k in range(4):
        pltpu.make_async_copy(normed_y.at[0:7], normed_y.at[0:7], ay_s.at[k]).wait()
    for g in range(5):
        n = 3 * len(groups[g])
        pltpu.make_async_copy(normed_z.at[0:n], normed_z.at[0:n], az_s.at[g]).wait()

    @pl.when(z < ZS - 1)
    def _():
        first_right().wait_send()

    @pl.when(z > 0)
    def _():
        first_left().wait_send()

    @pl.when(core == 0)
    def _():
        across_0().wait_send()
        for g in range(5):
            for i in groups[g]:
                own_z(g, i).wait_send()
        for i in range(1, 4):
            ring_up(i).wait_send()
            ring_down(i).wait_send()
        for k in range(3):
            z_copy(k).wait_send()

    @pl.when(core == 1)
    def _():
        across_1().wait_send()
        for k in range(4):
            own_y(k).wait_send()
        for h in (1, 2):

            @pl.when((z >= h) & (z < ZS - 1))
            def _():
                right(h).wait_send()

            @pl.when((z < ZS - h) & (z > 0))
            def _():
                left(h).wait_send()

        for s in range(4):
            up_copy(s).wait_send()
            down_copy(s).wait_send()


def finish(
    summed_hbm, total_hbm, weight_hbm, gain_hbm, global_hbm, momentum_hbm,
    local_out, gain_out, global_out, momentum_out,
    summed, total, weight, gain, outer, mom, local, gain_new, in_sem, out_sem,
):
    sources = (total_hbm, momentum_hbm, global_hbm, summed_hbm, weight_hbm.at[0], gain_hbm)
    loads = [
        pltpu.make_async_copy(src, dst, in_sem.at[i])
        for i, (src, dst) in enumerate(zip(sources, (total, mom, outer, summed, weight, gain)))
    ]
    for load in loads:
        load.start()
    for load in loads[:3]:
        load.wait()
    average = total[...] / 8.0
    mom[...] = 0.9 * mom[...] + average
    outer[...] = outer[...] - 0.7 * (average + 0.9 * mom[...])
    stores = [
        pltpu.make_async_copy(mom, momentum_out, out_sem.at[0]),
        pltpu.make_async_copy(outer, global_out, out_sem.at[1]),
    ]
    stores[0].start()
    stores[1].start()
    for load in loads[3:]:
        load.wait()
    eye = lax.broadcasted_iota(jnp.int32, (128, 128), 0) == lax.broadcasted_iota(
        jnp.int32, (128, 128), 1
    )
    root = math.sqrt(8192)
    held = weight[...].astype(F32)
    weight_grad = column(gain[...], eye) * summed[...] / root
    local[...] = 0.5 * (held - 0.2 * weight_grad) + 0.5 * outer[...]
    stores.append(pltpu.make_async_copy(local, local_out.at[0], out_sem.at[2]))
    stores[2].start()
    gain_grad = jnp.sum(held * summed[...], axis=1, keepdims=True) / root
    gain_row = jnp.sum(jnp.where(eye, gain_grad, 0.0), axis=0, keepdims=True)
    gain_new[...] = gain[...] - 0.005 * gain_row
    stores.append(pltpu.make_async_copy(gain_new, gain_out, out_sem.at[3]))
    stores[3].start()
    for store in stores:
        store.wait()


def shards(
    activations, cotangent, local_weight, norm_gain, global_weight, momentum, codes, exponents
):
    rows, width = global_weight.shape
    anywhere = pl.BlockSpec(memory_space=pl.ANY)
    sem = pltpu.SemaphoreType.DMA
    whole = jax.ShapeDtypeStruct((rows, width), F32)
    summed, total = pl.pallas_call(
        kernel,
        out_shape=(whole, whole),
        in_specs=[anywhere] * 4,
        out_specs=(anywhere,) * 2,
        scratch_shapes=[
            pltpu.VMEM((128, 8192), BF16),
            pltpu.VMEM((128, 512), BF16),
            pltpu.VMEM((32, 128, 128), BF16),
            pltpu.VMEM((32, 128, 128), BF16),
            pltpu.VMEM((4, 16, 128, 128), BF16),
            pltpu.VMEM((8, 8, 128, 128), BF16),
            pltpu.VMEM((8, 2, 128, 512), BF16),
            pltpu.VMEM((4, 2, 128, 512), BF16),
            pltpu.VMEM((128, 512), BF16),
            pltpu.VMEM((4, 128), jnp.int32),
            pltpu.VMEM((8, 128, 512), F32),
            pltpu.VMEM((3, 128, 512), F32),
            pltpu.VMEM((128, 256), F32),
            pltpu.VMEM((128, 256), F32),
            pltpu.VMEM((3, 128, 512), F32),
            pltpu.VMEM((3, 128, 512), F32),
            pltpu.VMEM((128, 512), BF16),
            pltpu.VMEM((3, 32, 512), BF16),
            pltpu.VMEM((32, 512), F32),
            pltpu.VMEM((32, 512), F32),
            pltpu.VMEM((128, 512), F32),
            sem((4,)),
            sem((2,)),
            sem((8,)),
            sem((9,)),
            sem((6,)),
            sem((7,)),
            sem((4,)),
            sem((4,)),
            sem((5,)),
            sem((5,)),
            sem((9,)),
            sem((3,)),
            sem((3,)),
            sem((4,)),
            sem((4,)),
            sem((4,)),
            sem((4,)),
            sem((3,)),
            sem((3,)),
            sem((1,)),
            sem((1,)),
            sem((3,)),
            sem((3,)),
        ],
        compiler_params=pltpu.CompilerParams(
            collective_id=0, has_side_effects=True, vmem_limit_bytes=60 << 20
        ),
        name="exchange",
    )(activations, cotangent, codes, jnp.transpose(exponents[0]))
    return pl.pallas_call(
        finish,
        out_shape=(
            jax.ShapeDtypeStruct((1, rows, width), F32),
            jax.ShapeDtypeStruct((1, rows), F32),
            whole,
            whole,
        ),
        in_specs=[anywhere] * 6,
        out_specs=(anywhere,) * 4,
        scratch_shapes=[
            pltpu.VMEM((128, 512), F32),
            pltpu.VMEM((128, 512), F32),
            pltpu.VMEM((128, 512), BF16),
            pltpu.VMEM((1, 128), F32),
            pltpu.VMEM((128, 512), F32),
            pltpu.VMEM((128, 512), F32),
            pltpu.VMEM((128, 512), F32),
            pltpu.VMEM((1, 128), F32),
            sem((6,)),
            sem((4,)),
        ],
        compiler_params=pltpu.CompilerParams(vmem_limit_bytes=60 << 20),
        name="finish",
    )(summed, total, local_weight, norm_gain, global_weight, momentum)


def solution(mesh):
    placed = (
        P("rep", "fsdp", None),
        P("rep", "fsdp", None),
        P("rep", "fsdp", None),
        P("rep", "fsdp"),
        P("fsdp", None),
        P("fsdp", None),
        P("rep", "fsdp", None),
        P("rep", "fsdp", None),
    )
    return jax.shard_map(
        shards,
        mesh=mesh,
        in_specs=placed,
        out_specs=(P("rep", "fsdp", None), P("rep", "fsdp"), P("fsdp", None), P("fsdp", None)),
        check_vma=False,
    )
```

```python
import functools
import math

import jax
import jax.numpy as jnp
from jax import lax
from jax.experimental import pallas as pl
from jax.experimental.pallas import tpu as pltpu
from jax.sharding import PartitionSpec as P

MESH = pl.DeviceIdType.MESH
YS, ZS, XS = 8, 4, 4
F32, BF16 = jnp.float32, jnp.bfloat16


def flip(value, mask):
    low, high = lax.rem(value, 2), value // 2
    if mask & 1:
        low = 1 - low
    if mask & 2:
        high = 1 - high
    return high * 2 + low


def column(row, eye):
    return jnp.sum(jnp.where(eye, row, 0.0), axis=1, keepdims=True)


def product(lhs, rhs):
    return lax.dot_general(lhs, rhs, (((0,), (0,)), ((), ())), preferred_element_type=F32)


def kernel(
    act_hbm, cot_hbm, codes_hbm, exps_hbm, summed_hbm, total_hbm,
    act, cot, normed_y, normed_z, recv_y, recv_z, cots_y, cots_z, codes, exps,
    part, from_z, ups, downs, decoded, x_in, x_sum, h_in, total,
    in_sem, out_sem, cy_s, cy_r, cz_s, cz_r, ay_s, ay_r, az_s, az_r, own_s,
    z_s, z_r, up_s, up_r, down_s, down_r, x1_s, x1_r, h_s, h_r, x2_s, x2_r, met,
):
    rep, pos = lax.axis_index("rep"), lax.axis_index("fsdp")
    zh, x = rep // XS, lax.rem(rep, XS)
    y, z, core = pos // (2 * ZS), lax.rem(pos // 2, ZS), lax.rem(pos, 2)
    width = act.shape[1]

    def at(yy=None, zz=None, cc=None, xx=None, hh=None):
        yy = y if yy is None else yy
        zz = z if zz is None else zz
        cc = core if cc is None else cc
        xx = x if xx is None else xx
        hh = zh if hh is None else hh
        return (hh * XS + xx, (yy * ZS + zz) * 2 + cc)

    def y_off(d):
        return lax.rem(y + d, YS)

    def x_off(d):
        return at(xx=lax.rem(x + d, XS))

    def send(src, dst, ssem, rsem, device):
        return pltpu.make_async_remote_copy(
            src_ref=src, dst_ref=dst, send_sem=ssem, recv_sem=rsem, device_id=device, device_id_type=MESH
        )

    def greet(device):
        pl.semaphore_signal(barrier, inc=1, device_id=device, device_id_type=MESH)

    other = at(hh=1 - zh)

    loads = [
        pltpu.make_async_copy(cot_hbm.at[0], cot, in_sem.at[0]),
        pltpu.make_async_copy(codes_hbm.at[0], codes, in_sem.at[1]),
        pltpu.make_async_copy(exps_hbm, exps, in_sem.at[2]),
        pltpu.make_async_copy(act_hbm.at[0], act, in_sem.at[3]),
    ]
    for load in loads:
        load.start()

    barrier = pltpu.get_barrier_semaphore()
    for device in [at(cc=1 - core)] + [x_off(d) for d in range(1, XS)]:
        greet(device)

    @pl.when(zh == 0)
    def _():
        greet(other)

    for q in (1, 2, 3):
        greet(at(zz=flip(z, q)))

    @pl.when(core == 0)
    def _():
        for d in range(1, YS):
            for c in range(2):
                greet(at(yy=y_off(d), cc=c))

    @pl.when(core == 1)
    def _():
        for q in (1, 2, 3):
            greet(at(zz=flip(z, q), cc=0))
        greet(at(yy=y_off(1)))
        greet(at(yy=y_off(7)))

    eye = lax.broadcasted_iota(jnp.int32, (128, 128), 0) == lax.broadcasted_iota(
        jnp.int32, (128, 128), 1
    )
    loads[1].wait()
    loads[2].wait()
    scales = jnp.exp2(exps[...].astype(F32))
    for b in range(4):
        cols = slice(b * 128, (b + 1) * 128)
        scale = column(scales[b : b + 1, :], eye)
        decoded[:, cols] = (codes[:, cols].astype(F32) * scale).astype(BF16)

    pl.semaphore_wait(barrier, 14 + zh + jnp.where(core == 0, 3, 2))

    @pl.when(zh == 1)
    def _():
        pl.semaphore_signal(met, inc=1, device_id=other, device_id_type=MESH)

    loads[0].wait()
    first = [
        send(cot, cots_y.at[1, core], cy_s.at[0], cy_r.at[0], at(yy=y_off(1), cc=0)),
        send(cot, cots_y.at[7, core], cy_s.at[4], cy_r.at[4], at(yy=y_off(7), cc=0)),
    ]
    for copy in first:
        copy.start()

    def first_right():
        return send(cot, cots_z.at[z, core], cz_s.at[0], cz_r.at[0], at(zz=z + 1, cc=1))

    def first_left():
        return send(cot, cots_z.at[z, core], cz_s.at[3], cz_r.at[3], at(zz=z - 1, cc=1))

    @pl.when(z < ZS - 1)
    def _():
        first_right().start()

    @pl.when(z > 0)
    def _():
        first_left().start()

    x_parts = []
    for d in range(1, XS):
        rows = pl.ds(pl.multiple_of(lax.rem(x + d, XS) * 32, 32), 32)
        x_parts.append(send(decoded.at[rows], x_in.at[d - 1], x1_s.at[d - 1], x1_r.at[d - 1], x_off(d)))
    for copy in x_parts:
        copy.start()

    def across_0():
        return send(cot, cots_z.at[z, 0], own_s.at[0], cz_r.at[6], at(cc=1))

    def across_1():
        return send(cot, cots_y.at[0, 1], own_s.at[0], cy_r.at[8], at(cc=0))

    @pl.when(core == 0)
    def _():
        across_0().start()
        cots_y[0, 0] = cot[...]

    @pl.when(core == 1)
    def _():
        across_1().start()
        cots_z[z, 1] = cot[...]

    loads[3].wait()

    @pl.loop(0, 8)
    def _(group):
        rows = pl.ds(pl.multiple_of(group * 16, 16), 16)
        squares = jnp.zeros((16, 256), F32)
        for b in range(32):
            values = act[rows, b * 256 : (b + 1) * 256].astype(F32)
            squares += values * values
        mean = jnp.sum(squares, axis=1, keepdims=True) / width
        scale = lax.rsqrt(mean + 1e-05)
        for b in range(32):
            values = act[rows, b * 256 : (b + 1) * 256].astype(F32)
            result = (values * scale).astype(BF16)
            normed_y[b, rows, :] = result[:, :128]
            normed_z[b // ZS + (b % ZS) * YS, rows, :] = result[:, 128:]

    def goal(k):
        if k == 0:
            return jnp.where(z < 2, 3, 0)
        if k == 1:
            return lax.rem(12 - 2 * z, 5)
        if k == 2:
            return 1 + lax.rem(z, 2)
        return z

    def push_y(k):
        zz = goal(k)
        for d in (4, 3, 5, 2, 6, 1, 7):
            yy = y_off(d)
            send(
                normed_y.at[yy * ZS + zz], recv_y.at[k, 2 * d + core], ay_s.at[k], ay_r.at[k], at(yy=yy, cc=0)
            ).start()

        @pl.when(core == 0)
        def _():
            recv_y[k, 0] = normed_y[y * ZS + zz]

        @pl.when(core == 1)
        def _():
            own_y(k).start()

    def own_y(k):
        zz = goal(k)
        return send(normed_y.at[y * ZS + zz], recv_y.at[k, 1], own_s.at[1 + k], ay_r.at[k], at(cc=0))

    def sent_y(k):
        pltpu.make_async_copy(normed_y.at[0:7], normed_y.at[0:7], ay_s.at[k]).wait()

    offsets = (4, 3, 5, 2, 6, 1, 7, 0)
    groups = ((0,), (1, 2), (3, 4), (5, 6), (7,))

    def push_z(g):
        for i in groups[g]:
            yy = y_off(offsets[i])
            for q in (3, 2, 1):
                zz = flip(z, q)
                send(
                    normed_z.at[zz * YS + yy], recv_z.at[i, z * 2 + core],
                    az_s.at[g], az_r.at[g], at(zz=zz, cc=1),
                ).start()

        @pl.when(core == 0)
        def _():
            for i in groups[g]:
                own_z(g, i).start()

        @pl.when(core == 1)
        def _():
            for i in groups[g]:
                recv_z[i, z * 2 + 1] = normed_z[z * YS + y_off(offsets[i])]

    def sent_z(g):
        n = 3 * len(groups[g])
        pltpu.make_async_copy(normed_z.at[0:n], normed_z.at[0:n], az_s.at[g]).wait()

    def own_z(g, i):
        return send(
            normed_z.at[z * YS + y_off(offsets[i])], recv_z.at[i, z * 2],
            own_s.at[1 + i], az_r.at[g], at(cc=1),
        )

    def z_copy(k):
        right = goal(k) > z
        slot = goal(k) + jnp.where(right, 0, 4)
        device = at(zz=z + jnp.where(right, 1, -1))
        return send(part.at[k], from_z.at[slot], z_s.at[k], z_r.at[slot], device)

    def inbox(slot):
        pltpu.make_async_copy(from_z.at[slot], from_z.at[slot], z_r.at[slot]).wait()
        return from_z[slot]

    def multiply_y(k):
        pltpu.make_async_copy(recv_y.at[k, 1:16], recv_y.at[k, 1:16], ay_r.at[k]).wait()
        part[k] = product(recv_y[k].reshape(2048, 128), cots_y[...].reshape(2048, 512))

    def pass_y(k):
        right = goal(k) > z

        @pl.when((right & (z > 0)) | (jnp.logical_not(right) & (z < ZS - 1)))
        def _():
            part[k] = part[k] + inbox(goal(k) + jnp.where(right, 0, 4))

        z_copy(k).start()

    def multiply_z(g):
        i, n = groups[g][0], len(groups[g])
        pltpu.make_async_copy(recv_z.at[i : i + n, 0:7], recv_z.at[i : i + n, 0:7], az_r.at[g]).wait()
        for i in groups[g]:
            part[i] = product(recv_z[i].reshape(1024, 128), cots_z[...].reshape(1024, 512))

    def up_copy(s, h):
        cols = slice(256 * h, 256 * h + 256)
        src = part.at[max(2 * s - 1, 0), :, cols]
        return send(src, ups.at[s, :, cols], up_s.at[s, h], up_r.at[s, h], at(yy=y_off(1)))

    def down_copy(s, h):
        cols = slice(256 * h, 256 * h + 256)
        src = part.at[2 * s, :, cols]
        return send(src, downs.at[s, :, cols], down_s.at[s, h], down_r.at[s, h], at(yy=y_off(7)))

    def add_up(s, h, i):
        if s > 0 or h == 0:
            cols = slice(256 * h, 256 * h + 256)
            up_copy(s, h).wait_recv()
            part[i, :, cols] = part[i, :, cols] + ups[s, :, cols]

    def add_down(s, h, i):
        if s > 0 or h == 1:
            cols = slice(256 * h, 256 * h + 256)
            down_copy(s, h).wait_recv()
            part[i, :, cols] = part[i, :, cols] + downs[s, :, cols]

    def chain(s):
        if s == 0:
            up_copy(0, 0).start()
            down_copy(0, 1).start()
        else:
            for h in range(2):
                add_up(s - 1, h, 2 * s - 1)
                up_copy(s, h).start()
                add_down(s - 1, h, 2 * s)
                down_copy(s, h).start()

    def ring_up(i):
        if i < 3:
            return send(cots_y.at[i], cots_y.at[i + 1], cy_s.at[i], cy_r.at[i], at(yy=y_off(1)))
        return send(cots_y.at[3, 0], cots_y.at[4, 0], cy_s.at[3], cy_r.at[3], at(yy=y_off(1)))

    def ring_down(i):
        if i < 3:
            return send(cots_y.at[8 - i], cots_y.at[7 - i], cy_s.at[4 + i], cy_r.at[4 + i], at(yy=y_off(7)))
        return send(cots_y.at[5, 1], cots_y.at[4, 1], cy_s.at[7], cy_r.at[7], at(yy=y_off(7)))

    def ring_wait(i):
        if i == 0:
            pltpu.make_async_copy(cots_y.at[1], cots_y.at[1], cy_r.at[0]).wait()
            pltpu.make_async_copy(cots_y.at[7], cots_y.at[7], cy_r.at[4]).wait()
        else:
            ring_up(i).wait_recv()
            ring_down(i).wait_recv()

    def ring_go(i):
        ring_up(i).start()
        ring_down(i).start()

    def right(h):
        return send(cots_z.at[z - h], cots_z.at[z - h], cz_s.at[h], cz_r.at[h], at(zz=z + 1))

    def left(h):
        return send(cots_z.at[z + h], cots_z.at[z + h], cz_s.at[3 + h], cz_r.at[3 + h], at(zz=z - 1))

    def line_wait(h):
        @pl.when(z >= h)
        def _():
            pltpu.make_async_copy(cots_z.at[0], cots_z.at[0], cz_r.at[h - 1]).wait()

        @pl.when(z < ZS - h)
        def _():
            pltpu.make_async_copy(cots_z.at[0], cots_z.at[0], cz_r.at[2 + h]).wait()

        if h < 3:

            @pl.when((z >= h) & (z < ZS - 1))
            def _():
                right(h).start()

            @pl.when((z < ZS - h) & (z > 0))
            def _():
                left(h).start()

    mine = pl.ds(pl.multiple_of(x * 32, 32), 32)
    h_copy = send(x_sum, h_in, h_s.at[0], h_r.at[0], other)
    totals = [
        send(total.at[mine], total.at[mine], x2_s.at[d - 1], x2_r.at[d - 1], x_off(d))
        for d in range(1, XS)
    ]

    def gather_x():
        for copy in x_parts:
            copy.wait_recv()
        x_sum[...] = (
            decoded[mine, :].astype(F32) + x_in[0].astype(F32) + x_in[1].astype(F32) + x_in[2].astype(F32)
        )

        @pl.when(zh == 0)
        def _():
            pl.semaphore_wait(met, 1)

        h_copy.start()

    def spread_total():
        h_copy.wait_recv()
        total[mine, :] = x_sum[...] + h_in[...]
        for copy in totals:
            copy.start()

    total_copy = pltpu.make_async_copy(total, total_hbm, out_sem.at[0])

    def write_total():
        for copy in totals:
            copy.wait_recv()
        total_copy.start()

    push_z(0)

    @pl.when(core == 0)
    def _():
        push_y(0)
        ring_wait(0)
        ring_go(1)
        sent_z(0)
        push_z(1)
        ring_wait(1)
        ring_go(2)
        push_y(1)
        gather_x()
        sent_z(1)
        push_z(2)
        ring_wait(2)
        ring_go(3)
        push_y(2)
        sent_z(2)
        push_z(3)
        across_1().wait_recv()
        ring_wait(3)
        multiply_y(0)
        pass_y(0)
        sent_y(1)
        push_y(3)
        sent_z(3)
        push_z(4)
        multiply_y(1)
        pass_y(1)
        spread_total()
        multiply_y(2)
        pass_y(2)
        write_total()
        multiply_y(3)
        @pl.when(z > 0)
        def _():
            part[3] = part[3] + inbox(z)

        @pl.when(z < ZS - 1)
        def _():
            part[3] = part[3] + inbox(z + 4)

        result = pltpu.make_async_copy(part.at[3], summed_hbm, out_sem.at[1])
        result.start()
        result.wait()
        sent_y(0)
        sent_y(2)
        sent_y(3)
        sent_z(4)

    @pl.when(core == 1)
    def _():
        line_wait(1)
        push_y(0)
        sent_z(0)
        push_z(1)
        line_wait(2)
        push_y(1)
        gather_x()
        sent_z(1)
        push_z(2)
        line_wait(3)
        across_0().wait_recv()
        multiply_z(0)
        chain(0)
        push_y(2)
        sent_z(2)
        push_z(3)
        multiply_z(1)
        chain(1)
        sent_z(3)
        push_z(4)
        push_y(3)
        multiply_z(2)
        chain(2)
        spread_total()
        multiply_z(3)
        chain(3)
        write_total()
        multiply_z(4)
        for h in range(2):
            add_up(3, h, 7)
            add_down(3, h, 7)
        result = pltpu.make_async_copy(part.at[7], summed_hbm, out_sem.at[1])
        result.start()
        result.wait()
        sent_y(0)
        sent_y(1)
        sent_y(2)
        sent_y(3)
        sent_z(4)

    total_copy.wait()
    for copy in first + x_parts + [h_copy] + totals:
        copy.wait_send()
    @pl.when(z < ZS - 1)
    def _():
        first_right().wait_send()

    @pl.when(z > 0)
    def _():
        first_left().wait_send()

    @pl.when(core == 0)
    def _():
        across_0().wait_send()
        for g in range(5):
            for i in groups[g]:
                own_z(g, i).wait_send()
        for i in range(1, 4):
            ring_up(i).wait_send()
            ring_down(i).wait_send()
        for k in range(3):
            z_copy(k).wait_send()

    @pl.when(core == 1)
    def _():
        across_1().wait_send()
        for k in range(4):
            own_y(k).wait_send()
        for h in (1, 2):

            @pl.when((z >= h) & (z < ZS - 1))
            def _():
                right(h).wait_send()

            @pl.when((z < ZS - h) & (z > 0))
            def _():
                left(h).wait_send()

        up_copy(0, 0).wait_send()
        down_copy(0, 1).wait_send()
        for s in range(1, 4):
            for h in range(2):
                up_copy(s, h).wait_send()
                down_copy(s, h).wait_send()


def finish(
    summed_hbm, total_hbm, weight_hbm, gain_hbm, global_hbm, momentum_hbm,
    local_out, gain_out, global_out, momentum_out,
    summed, total, weight, gain, outer, mom, local, gain_new, in_sem, out_sem,
):
    sources = (total_hbm, momentum_hbm, global_hbm, summed_hbm, weight_hbm.at[0], gain_hbm)
    loads = [
        pltpu.make_async_copy(src, dst, in_sem.at[i])
        for i, (src, dst) in enumerate(zip(sources, (total, mom, outer, summed, weight, gain)))
    ]
    for load in loads:
        load.start()
    for load in loads[:3]:
        load.wait()
    average = total[...] / 8.0
    mom[...] = 0.9 * mom[...] + average
    outer[...] = outer[...] - 0.7 * (average + 0.9 * mom[...])
    stores = [
        pltpu.make_async_copy(mom, momentum_out, out_sem.at[0]),
        pltpu.make_async_copy(outer, global_out, out_sem.at[1]),
    ]
    stores[0].start()
    stores[1].start()
    for load in loads[3:]:
        load.wait()
    eye = lax.broadcasted_iota(jnp.int32, (128, 128), 0) == lax.broadcasted_iota(
        jnp.int32, (128, 128), 1
    )
    root = math.sqrt(8192)
    held = weight[...].astype(F32)
    weight_grad = column(gain[...], eye) * summed[...] / root
    local[...] = 0.5 * (held - 0.2 * weight_grad) + 0.5 * outer[...]
    stores.append(pltpu.make_async_copy(local, local_out.at[0], out_sem.at[2]))
    stores[2].start()
    gain_grad = jnp.sum(held * summed[...], axis=1, keepdims=True) / root
    gain_row = jnp.sum(jnp.where(eye, gain_grad, 0.0), axis=0, keepdims=True)
    gain_new[...] = gain[...] - 0.005 * gain_row
    stores.append(pltpu.make_async_copy(gain_new, gain_out, out_sem.at[3]))
    stores[3].start()
    for store in stores:
        store.wait()


def shards(
    activations, cotangent, local_weight, norm_gain, global_weight, momentum, codes, exponents
):
    rows, width = global_weight.shape
    anywhere = pl.BlockSpec(memory_space=pl.ANY)
    sem = pltpu.SemaphoreType.DMA
    whole = jax.ShapeDtypeStruct((rows, width), F32)
    summed, total = pl.pallas_call(
        kernel,
        out_shape=(whole, whole),
        in_specs=[anywhere] * 4,
        out_specs=(anywhere,) * 2,
        scratch_shapes=[
            pltpu.VMEM((128, 8192), BF16),
            pltpu.VMEM((128, 512), BF16),
            pltpu.VMEM((32, 128, 128), BF16),
            pltpu.VMEM((32, 128, 128), BF16),
            pltpu.VMEM((4, 16, 128, 128), BF16),
            pltpu.VMEM((8, 8, 128, 128), BF16),
            pltpu.VMEM((8, 2, 128, 512), BF16),
            pltpu.VMEM((4, 2, 128, 512), BF16),
            pltpu.VMEM((128, 512), BF16),
            pltpu.VMEM((4, 128), jnp.int32),
            pltpu.VMEM((8, 128, 512), F32),
            pltpu.VMEM((7, 128, 512), F32),
            pltpu.VMEM((4, 128, 512), F32),
            pltpu.VMEM((4, 128, 512), F32),
            pltpu.VMEM((128, 512), BF16),
            pltpu.VMEM((3, 32, 512), BF16),
            pltpu.VMEM((32, 512), F32),
            pltpu.VMEM((32, 512), F32),
            pltpu.VMEM((128, 512), F32),
            sem((4,)),
            sem((2,)),
            sem((8,)),
            sem((9,)),
            sem((6,)),
            sem((7,)),
            sem((4,)),
            sem((4,)),
            sem((5,)),
            sem((5,)),
            sem((9,)),
            sem((3,)),
            sem((7,)),
            sem((4, 2)),
            sem((4, 2)),
            sem((4, 2)),
            sem((4, 2)),
            sem((3,)),
            sem((3,)),
            sem((1,)),
            sem((1,)),
            sem((3,)),
            sem((3,)),
            pltpu.SemaphoreType.REGULAR,
        ],
        compiler_params=pltpu.CompilerParams(
            collective_id=0, has_side_effects=True, vmem_limit_bytes=60 << 20
        ),
        name="exchange",
    )(activations, cotangent, codes, jnp.transpose(exponents[0]))
    return pl.pallas_call(
        finish,
        out_shape=(
            jax.ShapeDtypeStruct((1, rows, width), F32),
            jax.ShapeDtypeStruct((1, rows), F32),
            whole,
            whole,
        ),
        in_specs=[anywhere] * 6,
        out_specs=(anywhere,) * 4,
        scratch_shapes=[
            pltpu.VMEM((128, 512), F32),
            pltpu.VMEM((128, 512), F32),
            pltpu.VMEM((128, 512), BF16),
            pltpu.VMEM((1, 128), F32),
            pltpu.VMEM((128, 512), F32),
            pltpu.VMEM((128, 512), F32),
            pltpu.VMEM((128, 512), F32),
            pltpu.VMEM((1, 128), F32),
            sem((6,)),
            sem((4,)),
        ],
        compiler_params=pltpu.CompilerParams(vmem_limit_bytes=60 << 20),
        name="finish",
    )(summed, total, local_weight, norm_gain, global_weight, momentum)


def solution(mesh):
    placed = (
        P("rep", "fsdp", None),
        P("rep", "fsdp", None),
        P("rep", "fsdp", None),
        P("rep", "fsdp"),
        P("fsdp", None),
        P("fsdp", None),
        P("rep", "fsdp", None),
        P("rep", "fsdp", None),
    )
    return jax.shard_map(
        shards,
        mesh=mesh,
        in_specs=placed,
        out_specs=(P("rep", "fsdp", None), P("rep", "fsdp"), P("fsdp", None), P("fsdp", None)),
        check_vma=False,
    )
```

```python
import functools
import math

import jax
import jax.numpy as jnp
from jax import lax
from jax.experimental import pallas as pl
from jax.experimental.pallas import tpu as pltpu
from jax.sharding import PartitionSpec as P

MESH = pl.DeviceIdType.MESH
YS, ZS, XS = 8, 4, 4
F32, BF16 = jnp.float32, jnp.bfloat16


def flip(value, mask):
    low, high = lax.rem(value, 2), value // 2
    if mask & 1:
        low = 1 - low
    if mask & 2:
        high = 1 - high
    return high * 2 + low


def column(row, eye):
    return jnp.sum(jnp.where(eye, row, 0.0), axis=1, keepdims=True)


def product(lhs, rhs):
    return lax.dot_general(lhs, rhs, (((0,), (0,)), ((), ())), preferred_element_type=F32)


def kernel(
    act_hbm, cot_hbm, codes_hbm, exps_hbm, summed_hbm, total_hbm,
    act, cot, normed_y, normed_z, recv_y, recv_z, cots_y, cots_z, codes, exps,
    part, from_z, ups, downs, decoded, x_in, x_sum, h_in, total,
    in_sem, out_sem, cy_s, cy_r, cz_s, cz_r, ay_s, ay_r, az_s, az_r, own_s,
    z_s, z_r, up_s, up_r, down_s, down_r, x1_s, x1_r, h_s, h_r, x2_s, x2_r, met,
):
    rep, pos = lax.axis_index("rep"), lax.axis_index("fsdp")
    zh, x = rep // XS, lax.rem(rep, XS)
    y, z, core = pos // (2 * ZS), lax.rem(pos // 2, ZS), lax.rem(pos, 2)
    width = act.shape[1]

    def at(yy=None, zz=None, cc=None, xx=None, hh=None):
        yy = y if yy is None else yy
        zz = z if zz is None else zz
        cc = core if cc is None else cc
        xx = x if xx is None else xx
        hh = zh if hh is None else hh
        return (hh * XS + xx, (yy * ZS + zz) * 2 + cc)

    def y_off(d):
        return lax.rem(y + d, YS)

    def x_off(d):
        return at(xx=lax.rem(x + d, XS))

    def send(src, dst, ssem, rsem, device):
        return pltpu.make_async_remote_copy(
            src_ref=src, dst_ref=dst, send_sem=ssem, recv_sem=rsem, device_id=device, device_id_type=MESH
        )

    def greet(device):
        pl.semaphore_signal(barrier, inc=1, device_id=device, device_id_type=MESH)

    other = at(hh=1 - zh)

    loads = [
        pltpu.make_async_copy(cot_hbm.at[0], cot, in_sem.at[0]),
        pltpu.make_async_copy(act_hbm.at[0, 0:64], act.at[0:64], in_sem.at[3]),
        pltpu.make_async_copy(act_hbm.at[0, 64:128], act.at[64:128], in_sem.at[4]),
        pltpu.make_async_copy(codes_hbm.at[0], codes, in_sem.at[1]),
        pltpu.make_async_copy(exps_hbm, exps, in_sem.at[2]),
    ]
    for load in loads:
        load.start()

    barrier = pltpu.get_barrier_semaphore()
    for device in [at(cc=1 - core)] + [x_off(d) for d in range(1, XS)]:
        greet(device)

    @pl.when(zh == 0)
    def _():
        greet(other)

    for q in (1, 2, 3):
        greet(at(zz=flip(z, q)))

    @pl.when(core == 0)
    def _():
        for d in range(1, YS):
            for c in range(2):
                greet(at(yy=y_off(d), cc=c))

    @pl.when(core == 1)
    def _():
        for q in (1, 2, 3):
            greet(at(zz=flip(z, q), cc=0))
        greet(at(yy=y_off(1)))
        greet(at(yy=y_off(7)))

    pl.semaphore_wait(barrier, 14 + zh + jnp.where(core == 0, 3, 2))

    @pl.when(zh == 1)
    def _():
        pl.semaphore_signal(met, inc=1, device_id=other, device_id_type=MESH)

    loads[0].wait()
    first = [
        send(cot, cots_y.at[1, core], cy_s.at[0], cy_r.at[0], at(yy=y_off(1), cc=0)),
        send(cot, cots_y.at[7, core], cy_s.at[4], cy_r.at[4], at(yy=y_off(7), cc=0)),
    ]
    for copy in first:
        copy.start()

    def first_right():
        return send(cot, cots_z.at[z, core], cz_s.at[0], cz_r.at[0], at(zz=z + 1, cc=1))

    def first_left():
        return send(cot, cots_z.at[z, core], cz_s.at[3], cz_r.at[3], at(zz=z - 1, cc=1))

    @pl.when(z < ZS - 1)
    def _():
        first_right().start()

    @pl.when(z > 0)
    def _():
        first_left().start()

    def across_0():
        return send(cot, cots_z.at[z, 0], own_s.at[0], cz_r.at[6], at(cc=1))

    def across_1():
        return send(cot, cots_y.at[0, 1], own_s.at[0], cy_r.at[8], at(cc=0))

    @pl.when(core == 0)
    def _():
        across_0().start()
        cots_y[0, 0] = cot[...]

    @pl.when(core == 1)
    def _():
        across_1().start()
        cots_z[z, 1] = cot[...]

    def normalise(group):
        rows = pl.ds(pl.multiple_of(group * 16, 16), 16)
        squares = jnp.zeros((16, 256), F32)
        for b in range(32):
            values = act[rows, b * 256 : (b + 1) * 256].astype(F32)
            squares += values * values
        mean = jnp.sum(squares, axis=1, keepdims=True) / width
        scale = lax.rsqrt(mean + 1e-05)
        for b in range(32):
            values = act[rows, b * 256 : (b + 1) * 256].astype(F32)
            result = (values * scale).astype(BF16)
            normed_y[b, rows, :] = result[:, :128]
            normed_z[b // ZS + (b % ZS) * YS, rows, :] = result[:, 128:]

    loads[1].wait()
    pl.loop(0, 4)(normalise)
    loads[2].wait()
    pl.loop(4, 8)(normalise)

    def goal(k):
        if k == 0:
            return jnp.where(z < 2, 3, 0)
        if k == 1:
            return lax.rem(12 - 2 * z, 5)
        if k == 2:
            return 1 + lax.rem(z, 2)
        return z

    def push_y(k, steps=(4, 3, 5, 2, 6, 1, 7)):
        zz = goal(k)
        for d in steps:
            yy = y_off(d)
            send(
                normed_y.at[yy * ZS + zz], recv_y.at[k, 2 * d + core], ay_s.at[k], ay_r.at[k], at(yy=yy, cc=0)
            ).start()

        if 1 not in steps:
            return

        @pl.when(core == 0)
        def _():
            recv_y[k, 0] = normed_y[y * ZS + zz]

        @pl.when(core == 1)
        def _():
            own_y(k).start()

    def own_y(k):
        zz = goal(k)
        return send(normed_y.at[y * ZS + zz], recv_y.at[k, 1], own_s.at[1 + k], ay_r.at[k], at(cc=0))

    def sent_y(k):
        pltpu.make_async_copy(normed_y.at[0:7], normed_y.at[0:7], ay_s.at[k]).wait()

    offsets = (4, 3, 5, 2, 6, 1, 7, 0)
    groups = ((0,), (1, 2), (3, 4), (5, 6), (7,))

    def push_z(g):
        for i in groups[g]:
            yy = y_off(offsets[i])
            for q in (3, 2, 1):
                zz = flip(z, q)
                send(
                    normed_z.at[zz * YS + yy], recv_z.at[i, z * 2 + core],
                    az_s.at[g], az_r.at[g], at(zz=zz, cc=1),
                ).start()

        @pl.when(core == 0)
        def _():
            for i in groups[g]:
                own_z(g, i).start()

        @pl.when(core == 1)
        def _():
            for i in groups[g]:
                recv_z[i, z * 2 + 1] = normed_z[z * YS + y_off(offsets[i])]

    def sent_z(g):
        n = 3 * len(groups[g])
        pltpu.make_async_copy(normed_z.at[0:n], normed_z.at[0:n], az_s.at[g]).wait()

    def own_z(g, i):
        return send(
            normed_z.at[z * YS + y_off(offsets[i])], recv_z.at[i, z * 2],
            own_s.at[1 + i], az_r.at[g], at(cc=1),
        )

    def z_copy(k):
        right = goal(k) > z
        slot = goal(k) + jnp.where(right, 0, 4)
        device = at(zz=z + jnp.where(right, 1, -1))
        return send(part.at[k], from_z.at[slot], z_s.at[k], z_r.at[slot], device)

    def inbox(slot):
        pltpu.make_async_copy(from_z.at[slot], from_z.at[slot], z_r.at[slot]).wait()
        return from_z[slot]

    def multiply_y(k):
        pltpu.make_async_copy(recv_y.at[k, 1:16], recv_y.at[k, 1:16], ay_r.at[k]).wait()
        part[k] = product(recv_y[k].reshape(2048, 128), cots_y[...].reshape(2048, 512))

    def pass_y(k):
        right = goal(k) > z

        @pl.when((right & (z > 0)) | (jnp.logical_not(right) & (z < ZS - 1)))
        def _():
            part[k] = part[k] + inbox(goal(k) + jnp.where(right, 0, 4))

        z_copy(k).start()

    def multiply_z(g):
        i, n = groups[g][0], len(groups[g])
        pltpu.make_async_copy(recv_z.at[i : i + n, 0:7], recv_z.at[i : i + n, 0:7], az_r.at[g]).wait()
        for i in groups[g]:
            part[i] = product(recv_z[i].reshape(1024, 128), cots_z[...].reshape(1024, 512))

    def up_copy(s, h):
        cols = slice(256 * h, 256 * h + 256)
        src = part.at[max(2 * s - 1, 0), :, cols]
        return send(src, ups.at[s, :, cols], up_s.at[s, h], up_r.at[s, h], at(yy=y_off(1)))

    def down_copy(s, h):
        cols = slice(256 * h, 256 * h + 256)
        src = part.at[2 * s, :, cols]
        return send(src, downs.at[s, :, cols], down_s.at[s, h], down_r.at[s, h], at(yy=y_off(7)))

    def add_up(s, h, i):
        if s > 0 or h == 0:
            cols = slice(256 * h, 256 * h + 256)
            up_copy(s, h).wait_recv()
            part[i, :, cols] = part[i, :, cols] + ups[s, :, cols]

    def add_down(s, h, i):
        if s > 0 or h == 1:
            cols = slice(256 * h, 256 * h + 256)
            down_copy(s, h).wait_recv()
            part[i, :, cols] = part[i, :, cols] + downs[s, :, cols]

    def chain(s):
        if s == 0:
            up_copy(0, 0).start()
            down_copy(0, 1).start()
        else:
            for h in range(2):
                add_up(s - 1, h, 2 * s - 1)
                up_copy(s, h).start()
                add_down(s - 1, h, 2 * s)
                down_copy(s, h).start()

    def ring_up(i):
        if i < 3:
            return send(cots_y.at[i], cots_y.at[i + 1], cy_s.at[i], cy_r.at[i], at(yy=y_off(1)))
        return send(cots_y.at[3, 0], cots_y.at[4, 0], cy_s.at[3], cy_r.at[3], at(yy=y_off(1)))

    def ring_down(i):
        if i < 3:
            return send(cots_y.at[8 - i], cots_y.at[7 - i], cy_s.at[4 + i], cy_r.at[4 + i], at(yy=y_off(7)))
        return send(cots_y.at[5, 1], cots_y.at[4, 1], cy_s.at[7], cy_r.at[7], at(yy=y_off(7)))

    def ring_wait(i):
        if i == 0:
            pltpu.make_async_copy(cots_y.at[1], cots_y.at[1], cy_r.at[0]).wait()
            pltpu.make_async_copy(cots_y.at[7], cots_y.at[7], cy_r.at[4]).wait()
        else:
            ring_up(i).wait_recv()
            ring_down(i).wait_recv()

    def ring_go(i):
        ring_up(i).start()
        ring_down(i).start()

    def right(h):
        return send(cots_z.at[z - h], cots_z.at[z - h], cz_s.at[h], cz_r.at[h], at(zz=z + 1))

    def left(h):
        return send(cots_z.at[z + h], cots_z.at[z + h], cz_s.at[3 + h], cz_r.at[3 + h], at(zz=z - 1))

    def line_wait(h):
        @pl.when(z >= h)
        def _():
            pltpu.make_async_copy(cots_z.at[0], cots_z.at[0], cz_r.at[h - 1]).wait()

        @pl.when(z < ZS - h)
        def _():
            pltpu.make_async_copy(cots_z.at[0], cots_z.at[0], cz_r.at[2 + h]).wait()

        if h < 3:

            @pl.when((z >= h) & (z < ZS - 1))
            def _():
                right(h).start()

            @pl.when((z < ZS - h) & (z > 0))
            def _():
                left(h).start()

    mine = pl.ds(pl.multiple_of(x * 32, 32), 32)
    h_copy = send(x_sum, h_in, h_s.at[0], h_r.at[0], other)
    totals = [
        send(total.at[mine], total.at[mine], x2_s.at[d - 1], x2_r.at[d - 1], x_off(d))
        for d in range(1, XS)
    ]

    x_parts = []
    for d in range(1, XS):
        rows = pl.ds(pl.multiple_of(lax.rem(x + d, XS) * 32, 32), 32)
        x_parts.append(send(decoded.at[rows], x_in.at[d - 1], x1_s.at[d - 1], x1_r.at[d - 1], x_off(d)))

    def share_codes():
        eye = lax.broadcasted_iota(jnp.int32, (128, 128), 0) == lax.broadcasted_iota(
            jnp.int32, (128, 128), 1
        )
        loads[3].wait()
        loads[4].wait()
        scales = jnp.exp2(exps[...].astype(F32))
        for b in range(4):
            cols = slice(b * 128, (b + 1) * 128)
            scale = column(scales[b : b + 1, :], eye)
            decoded[:, cols] = (codes[:, cols].astype(F32) * scale).astype(BF16)
        for copy in x_parts:
            copy.start()

    def gather_x():
        for copy in x_parts:
            copy.wait_recv()
        x_sum[...] = (
            decoded[mine, :].astype(F32) + x_in[0].astype(F32) + x_in[1].astype(F32) + x_in[2].astype(F32)
        )

        @pl.when(zh == 0)
        def _():
            pl.semaphore_wait(met, 1)

        h_copy.start()

    def spread_total():
        h_copy.wait_recv()
        total[mine, :] = x_sum[...] + h_in[...]
        for copy in totals:
            copy.start()

    total_copy = pltpu.make_async_copy(total, total_hbm, out_sem.at[0])

    def write_total():
        for copy in totals:
            copy.wait_recv()
        total_copy.start()

    push_z(0)

    @pl.when(core == 0)
    def _():
        push_y(0, (4, 3, 5))
        ring_wait(0)
        ring_go(1)
        push_y(0, (2, 6, 1, 7))
        share_codes()
        sent_z(0)
        push_z(1)
        push_y(1, (4, 3, 5))
        ring_wait(1)
        ring_go(2)
        push_y(1, (2, 6, 1, 7))
        gather_x()
        sent_z(1)
        push_z(2)
        push_y(2, (4, 3, 5))
        ring_wait(2)
        ring_go(3)
        push_y(2, (2, 6, 1, 7))
        sent_z(2)
        push_z(3)
        push_y(3, (4, 3, 5))
        across_1().wait_recv()
        ring_wait(3)
        multiply_y(0)
        push_y(3, (2, 6, 1, 7))
        pass_y(0)
        sent_z(3)
        push_z(4)
        multiply_y(1)
        pass_y(1)
        spread_total()
        multiply_y(2)
        pass_y(2)
        write_total()
        multiply_y(3)
        @pl.when(z > 0)
        def _():
            part[3] = part[3] + inbox(z)

        @pl.when(z < ZS - 1)
        def _():
            part[3] = part[3] + inbox(z + 4)

        result = pltpu.make_async_copy(part.at[3], summed_hbm, out_sem.at[1])
        result.start()
        result.wait()
        sent_y(0)
        sent_y(1)
        sent_y(2)
        sent_y(3)
        sent_z(4)

    @pl.when(core == 1)
    def _():
        line_wait(1)
        push_y(0)
        share_codes()
        sent_z(0)
        push_z(1)
        push_y(1, (4, 3, 5))
        line_wait(2)
        push_y(1, (2, 6, 1, 7))
        gather_x()
        sent_z(1)
        push_z(2)
        line_wait(3)
        across_0().wait_recv()
        multiply_z(0)
        chain(0)
        sent_z(2)
        push_z(3)
        push_y(2)
        multiply_z(1)
        chain(1)
        sent_z(3)
        push_z(4)
        push_y(3)
        multiply_z(2)
        chain(2)
        spread_total()
        multiply_z(3)
        chain(3)
        write_total()
        multiply_z(4)
        for h in range(2):
            add_up(3, h, 7)
            add_down(3, h, 7)
        result = pltpu.make_async_copy(part.at[7], summed_hbm, out_sem.at[1])
        result.start()
        result.wait()
        sent_y(0)
        sent_y(1)
        sent_y(2)
        sent_y(3)
        sent_z(4)

    total_copy.wait()
    for copy in first + x_parts + [h_copy] + totals:
        copy.wait_send()
    @pl.when(z < ZS - 1)
    def _():
        first_right().wait_send()

    @pl.when(z > 0)
    def _():
        first_left().wait_send()

    @pl.when(core == 0)
    def _():
        across_0().wait_send()
        for g in range(5):
            for i in groups[g]:
                own_z(g, i).wait_send()
        for i in range(1, 4):
            ring_up(i).wait_send()
            ring_down(i).wait_send()
        for k in range(3):
            z_copy(k).wait_send()

    @pl.when(core == 1)
    def _():
        across_1().wait_send()
        for k in range(4):
            own_y(k).wait_send()
        for h in (1, 2):

            @pl.when((z >= h) & (z < ZS - 1))
            def _():
                right(h).wait_send()

            @pl.when((z < ZS - h) & (z > 0))
            def _():
                left(h).wait_send()

        up_copy(0, 0).wait_send()
        down_copy(0, 1).wait_send()
        for s in range(1, 4):
            for h in range(2):
                up_copy(s, h).wait_send()
                down_copy(s, h).wait_send()


def finish(
    summed_hbm, total_hbm, weight_hbm, gain_hbm, global_hbm, momentum_hbm,
    local_out, gain_out, global_out, momentum_out,
    summed, total, weight, gain, outer, mom, local, gain_new, in_sem, out_sem,
):
    sources = (total_hbm, momentum_hbm, global_hbm, summed_hbm, weight_hbm.at[0], gain_hbm)
    loads = [
        pltpu.make_async_copy(src, dst, in_sem.at[i])
        for i, (src, dst) in enumerate(zip(sources, (total, mom, outer, summed, weight, gain)))
    ]
    for load in loads:
        load.start()
    for load in loads[:3]:
        load.wait()
    average = total[...] / 8.0
    mom[...] = 0.9 * mom[...] + average
    outer[...] = outer[...] - 0.7 * (average + 0.9 * mom[...])
    stores = [
        pltpu.make_async_copy(mom, momentum_out, out_sem.at[0]),
        pltpu.make_async_copy(outer, global_out, out_sem.at[1]),
    ]
    stores[0].start()
    stores[1].start()
    for load in loads[3:]:
        load.wait()
    eye = lax.broadcasted_iota(jnp.int32, (128, 128), 0) == lax.broadcasted_iota(
        jnp.int32, (128, 128), 1
    )
    root = math.sqrt(8192)
    held = weight[...].astype(F32)
    weight_grad = column(gain[...], eye) * summed[...] / root
    local[...] = 0.5 * (held - 0.2 * weight_grad) + 0.5 * outer[...]
    stores.append(pltpu.make_async_copy(local, local_out.at[0], out_sem.at[2]))
    stores[2].start()
    gain_grad = jnp.sum(held * summed[...], axis=1, keepdims=True) / root
    gain_row = jnp.sum(jnp.where(eye, gain_grad, 0.0), axis=0, keepdims=True)
    gain_new[...] = gain[...] - 0.005 * gain_row
    stores.append(pltpu.make_async_copy(gain_new, gain_out, out_sem.at[3]))
    stores[3].start()
    for store in stores:
        store.wait()


def shards(
    activations, cotangent, local_weight, norm_gain, global_weight, momentum, codes, exponents
):
    rows, width = global_weight.shape
    anywhere = pl.BlockSpec(memory_space=pl.ANY)
    sem = pltpu.SemaphoreType.DMA
    whole = jax.ShapeDtypeStruct((rows, width), F32)
    summed, total = pl.pallas_call(
        kernel,
        out_shape=(whole, whole),
        in_specs=[anywhere] * 4,
        out_specs=(anywhere,) * 2,
        scratch_shapes=[
            pltpu.VMEM((128, 8192), BF16),
            pltpu.VMEM((128, 512), BF16),
            pltpu.VMEM((32, 128, 128), BF16),
            pltpu.VMEM((32, 128, 128), BF16),
            pltpu.VMEM((4, 16, 128, 128), BF16),
            pltpu.VMEM((8, 8, 128, 128), BF16),
            pltpu.VMEM((8, 2, 128, 512), BF16),
            pltpu.VMEM((4, 2, 128, 512), BF16),
            pltpu.VMEM((128, 512), BF16),
            pltpu.VMEM((4, 128), jnp.int32),
            pltpu.VMEM((8, 128, 512), F32),
            pltpu.VMEM((7, 128, 512), F32),
            pltpu.VMEM((4, 128, 512), F32),
            pltpu.VMEM((4, 128, 512), F32),
            pltpu.VMEM((128, 512), BF16),
            pltpu.VMEM((3, 32, 512), BF16),
            pltpu.VMEM((32, 512), F32),
            pltpu.VMEM((32, 512), F32),
            pltpu.VMEM((128, 512), F32),
            sem((5,)),
            sem((2,)),
            sem((8,)),
            sem((9,)),
            sem((6,)),
            sem((7,)),
            sem((4,)),
            sem((4,)),
            sem((5,)),
            sem((5,)),
            sem((9,)),
            sem((3,)),
            sem((7,)),
            sem((4, 2)),
            sem((4, 2)),
            sem((4, 2)),
            sem((4, 2)),
            sem((3,)),
            sem((3,)),
            sem((1,)),
            sem((1,)),
            sem((3,)),
            sem((3,)),
            pltpu.SemaphoreType.REGULAR,
        ],
        compiler_params=pltpu.CompilerParams(
            collective_id=0, has_side_effects=True, vmem_limit_bytes=60 << 20
        ),
        name="exchange",
    )(activations, cotangent, codes, jnp.transpose(exponents[0]))
    return pl.pallas_call(
        finish,
        out_shape=(
            jax.ShapeDtypeStruct((1, rows, width), F32),
            jax.ShapeDtypeStruct((1, rows), F32),
            whole,
            whole,
        ),
        in_specs=[anywhere] * 6,
        out_specs=(anywhere,) * 4,
        scratch_shapes=[
            pltpu.VMEM((128, 512), F32),
            pltpu.VMEM((128, 512), F32),
            pltpu.VMEM((128, 512), BF16),
            pltpu.VMEM((1, 128), F32),
            pltpu.VMEM((128, 512), F32),
            pltpu.VMEM((128, 512), F32),
            pltpu.VMEM((128, 512), F32),
            pltpu.VMEM((1, 128), F32),
            sem((6,)),
            sem((4,)),
        ],
        compiler_params=pltpu.CompilerParams(vmem_limit_bytes=60 << 20),
        name="finish",
    )(summed, total, local_weight, norm_gain, global_weight, momentum)


def solution(mesh):
    placed = (
        P("rep", "fsdp", None),
        P("rep", "fsdp", None),
        P("rep", "fsdp", None),
        P("rep", "fsdp"),
        P("fsdp", None),
        P("fsdp", None),
        P("rep", "fsdp", None),
        P("rep", "fsdp", None),
    )
    return jax.shard_map(
        shards,
        mesh=mesh,
        in_specs=placed,
        out_specs=(P("rep", "fsdp", None), P("rep", "fsdp"), P("fsdp", None), P("fsdp", None)),
        check_vma=False,
    )
```

```python
import functools
import math

import jax
import jax.numpy as jnp
from jax import lax
from jax.experimental import pallas as pl
from jax.experimental.pallas import tpu as pltpu
from jax.sharding import PartitionSpec as P

MESH = pl.DeviceIdType.MESH
YS, ZS, XS = 8, 4, 4
F32, BF16 = jnp.float32, jnp.bfloat16


def flip(value, mask):
    low, high = lax.rem(value, 2), value // 2
    if mask & 1:
        low = 1 - low
    if mask & 2:
        high = 1 - high
    return high * 2 + low


def column(row, eye):
    return jnp.sum(jnp.where(eye, row, 0.0), axis=1, keepdims=True)


def product(lhs, rhs):
    return lax.dot_general(lhs, rhs, (((0,), (0,)), ((), ())), preferred_element_type=F32)


def kernel(
    act_hbm, cot_hbm, codes_hbm, exps_hbm, summed_hbm, total_hbm,
    act, cot, normed_y, normed_z, recv_y, recv_z, cots_y, cots_z, codes, exps,
    part, from_z, ups, downs, decoded, x_in, x_sum, h_in, total,
    in_sem, out_sem, cy_s, cy_r, cz_s, cz_r, ay_s, ay_r, az_s, az_r, own_s,
    z_s, z_r, up_s, up_r, down_s, down_r, x1_s, x1_r, h_s, h_r, x2_s, x2_r, met,
):
    rep, pos = lax.axis_index("rep"), lax.axis_index("fsdp")
    zh, x = rep // XS, lax.rem(rep, XS)
    y, z, core = pos // (2 * ZS), lax.rem(pos // 2, ZS), lax.rem(pos, 2)
    width = act.shape[1]

    def at(yy=None, zz=None, cc=None, xx=None, hh=None):
        yy = y if yy is None else yy
        zz = z if zz is None else zz
        cc = core if cc is None else cc
        xx = x if xx is None else xx
        hh = zh if hh is None else hh
        return (hh * XS + xx, (yy * ZS + zz) * 2 + cc)

    def y_off(d):
        return lax.rem(y + d, YS)

    def x_off(d):
        return at(xx=lax.rem(x + d, XS))

    def send(src, dst, ssem, rsem, device):
        return pltpu.make_async_remote_copy(
            src_ref=src, dst_ref=dst, send_sem=ssem, recv_sem=rsem, device_id=device, device_id_type=MESH
        )

    def greet(device):
        pl.semaphore_signal(barrier, inc=1, device_id=device, device_id_type=MESH)

    other = at(hh=1 - zh)

    loads = [
        pltpu.make_async_copy(cot_hbm.at[0], cot, in_sem.at[0]),
        pltpu.make_async_copy(act_hbm.at[0, 0:64], act.at[0:64], in_sem.at[3]),
        pltpu.make_async_copy(act_hbm.at[0, 64:128], act.at[64:128], in_sem.at[4]),
        pltpu.make_async_copy(codes_hbm.at[0], codes, in_sem.at[1]),
        pltpu.make_async_copy(exps_hbm, exps, in_sem.at[2]),
    ]
    for load in loads:
        load.start()

    barrier = pltpu.get_barrier_semaphore()
    for device in [at(cc=1 - core)] + [x_off(d) for d in range(1, XS)]:
        greet(device)

    @pl.when(zh == 0)
    def _():
        greet(other)

    for q in (1, 2, 3):
        greet(at(zz=flip(z, q)))

    @pl.when(core == 0)
    def _():
        for d in range(1, YS):
            for c in range(2):
                greet(at(yy=y_off(d), cc=c))

    @pl.when(core == 1)
    def _():
        for q in (1, 2, 3):
            greet(at(zz=flip(z, q), cc=0))
        greet(at(yy=y_off(1)))
        greet(at(yy=y_off(7)))

    pl.semaphore_wait(barrier, 14 + zh + jnp.where(core == 0, 3, 2))

    @pl.when(zh == 1)
    def _():
        pl.semaphore_signal(met, inc=1, device_id=other, device_id_type=MESH)

    loads[0].wait()
    first = [
        send(cot, cots_y.at[1, core], cy_s.at[0], cy_r.at[0], at(yy=y_off(1), cc=0)),
        send(cot, cots_y.at[7, core], cy_s.at[4], cy_r.at[4], at(yy=y_off(7), cc=0)),
    ]
    for copy in first:
        copy.start()

    def first_right():
        return send(cot, cots_z.at[z, core], cz_s.at[0], cz_r.at[0], at(zz=z + 1, cc=1))

    def first_left():
        return send(cot, cots_z.at[z, core], cz_s.at[3], cz_r.at[3], at(zz=z - 1, cc=1))

    @pl.when(z < ZS - 1)
    def _():
        first_right().start()

    @pl.when(z > 0)
    def _():
        first_left().start()

    def across_0():
        return send(cot, cots_z.at[z, 0], own_s.at[0], cz_r.at[6], at(cc=1))

    def across_1():
        return send(cot, cots_y.at[0, 1], own_s.at[0], cy_r.at[8], at(cc=0))

    @pl.when(core == 0)
    def _():
        across_0().start()
        cots_y[0, 0] = cot[...]

    @pl.when(core == 1)
    def _():
        across_1().start()
        cots_z[z, 1] = cot[...]

    def normalise(group):
        rows = pl.ds(pl.multiple_of(group * 16, 16), 16)
        squares = jnp.zeros((16, 256), F32)
        for b in range(32):
            values = act[rows, b * 256 : (b + 1) * 256].astype(F32)
            squares += values * values
        mean = jnp.sum(squares, axis=1, keepdims=True) / width
        scale = lax.rsqrt(mean + 1e-05)
        for b in range(32):
            values = act[rows, b * 256 : (b + 1) * 256].astype(F32)
            result = (values * scale).astype(BF16)
            normed_y[b, rows, :] = result[:, :128]
            normed_z[b // ZS + (b % ZS) * YS, rows, :] = result[:, 128:]

    loads[1].wait()
    pl.loop(0, 4)(normalise)
    loads[2].wait()
    pl.loop(4, 8)(normalise)

    def goal(k):
        if k == 0:
            return jnp.where(z < 2, 3, 0)
        if k == 1:
            return lax.rem(12 - 2 * z, 5)
        if k == 2:
            return 1 + lax.rem(z, 2)
        return z

    def push_y(k, steps=(4, 3, 5, 2, 6, 1, 7)):
        zz = goal(k)
        for d in steps:
            yy = y_off(d)
            send(
                normed_y.at[yy * ZS + zz], recv_y.at[k, 2 * d + core], ay_s.at[k], ay_r.at[k], at(yy=yy, cc=0)
            ).start()

        if 1 not in steps:
            return

        @pl.when(core == 0)
        def _():
            recv_y[k, 0] = normed_y[y * ZS + zz]

        @pl.when(core == 1)
        def _():
            own_y(k).start()

    def own_y(k):
        zz = goal(k)
        return send(normed_y.at[y * ZS + zz], recv_y.at[k, 1], own_s.at[1 + k], ay_r.at[k], at(cc=0))

    def sent_y(k):
        pltpu.make_async_copy(normed_y.at[0:7], normed_y.at[0:7], ay_s.at[k]).wait()

    offsets = (4, 3, 5, 2, 6, 1, 7, 0)
    groups = ((0,), (1, 2), (3, 4), (5, 6), (7,))

    def push_z(g):
        for i in groups[g]:
            yy = y_off(offsets[i])
            for q in (3, 2, 1):
                zz = flip(z, q)
                send(
                    normed_z.at[zz * YS + yy], recv_z.at[i, z * 2 + core],
                    az_s.at[g], az_r.at[g], at(zz=zz, cc=1),
                ).start()

        @pl.when(core == 0)
        def _():
            for i in groups[g]:
                own_z(g, i).start()

        @pl.when(core == 1)
        def _():
            for i in groups[g]:
                recv_z[i, z * 2 + 1] = normed_z[z * YS + y_off(offsets[i])]

    def sent_z(g):
        n = 3 * len(groups[g])
        pltpu.make_async_copy(normed_z.at[0:n], normed_z.at[0:n], az_s.at[g]).wait()

    def own_z(g, i):
        return send(
            normed_z.at[z * YS + y_off(offsets[i])], recv_z.at[i, z * 2],
            own_s.at[1 + i], az_r.at[g], at(cc=1),
        )

    def z_copy(k):
        right = goal(k) > z
        slot = goal(k) + jnp.where(right, 0, 4)
        device = at(zz=z + jnp.where(right, 1, -1))
        return send(part.at[k], from_z.at[slot], z_s.at[k], z_r.at[slot], device)

    def inbox(slot):
        pltpu.make_async_copy(from_z.at[slot], from_z.at[slot], z_r.at[slot]).wait()
        return from_z[slot]

    def multiply_y(k):
        pltpu.make_async_copy(recv_y.at[k, 1:16], recv_y.at[k, 1:16], ay_r.at[k]).wait()
        part[k] = product(recv_y[k].reshape(2048, 128), cots_y[...].reshape(2048, 512))

    def pass_y(k):
        right = goal(k) > z

        @pl.when((right & (z > 0)) | (jnp.logical_not(right) & (z < ZS - 1)))
        def _():
            part[k] = part[k] + inbox(goal(k) + jnp.where(right, 0, 4))

        z_copy(k).start()

    def multiply_z(g):
        i, n = groups[g][0], len(groups[g])
        pltpu.make_async_copy(recv_z.at[i : i + n, 0:7], recv_z.at[i : i + n, 0:7], az_r.at[g]).wait()
        for i in groups[g]:
            part[i] = product(recv_z[i].reshape(1024, 128), cots_z[...].reshape(1024, 512))

    def up_copy(s, h):
        cols = slice(256 * h, 256 * h + 256)
        src = part.at[max(2 * s - 1, 0), :, cols]
        return send(src, ups.at[s, :, cols], up_s.at[s, h], up_r.at[s, h], at(yy=y_off(1)))

    def down_copy(s, h):
        cols = slice(256 * h, 256 * h + 256)
        src = part.at[2 * s, :, cols]
        return send(src, downs.at[s, :, cols], down_s.at[s, h], down_r.at[s, h], at(yy=y_off(7)))

    def add_up(s, h, i):
        if s > 0 or h == 0:
            cols = slice(256 * h, 256 * h + 256)
            up_copy(s, h).wait_recv()
            part[i, :, cols] = part[i, :, cols] + ups[s, :, cols]

    def add_down(s, h, i):
        if s > 0 or h == 1:
            cols = slice(256 * h, 256 * h + 256)
            down_copy(s, h).wait_recv()
            part[i, :, cols] = part[i, :, cols] + downs[s, :, cols]

    def chain(s):
        if s == 0:
            up_copy(0, 0).start()
            down_copy(0, 1).start()
        else:
            for h in range(2):
                add_up(s - 1, h, 2 * s - 1)
                up_copy(s, h).start()
                add_down(s - 1, h, 2 * s)
                down_copy(s, h).start()

    def ring_up(i):
        if i < 3:
            return send(cots_y.at[i], cots_y.at[i + 1], cy_s.at[i], cy_r.at[i], at(yy=y_off(1)))
        return send(cots_y.at[3, 0], cots_y.at[4, 0], cy_s.at[3], cy_r.at[3], at(yy=y_off(1)))

    def ring_down(i):
        if i < 3:
            return send(cots_y.at[8 - i], cots_y.at[7 - i], cy_s.at[4 + i], cy_r.at[4 + i], at(yy=y_off(7)))
        return send(cots_y.at[5, 1], cots_y.at[4, 1], cy_s.at[7], cy_r.at[7], at(yy=y_off(7)))

    def ring_wait(i):
        if i == 0:
            pltpu.make_async_copy(cots_y.at[1], cots_y.at[1], cy_r.at[0]).wait()
            pltpu.make_async_copy(cots_y.at[7], cots_y.at[7], cy_r.at[4]).wait()
        else:
            ring_up(i).wait_recv()
            ring_down(i).wait_recv()

    def ring_go(i):
        ring_up(i).start()
        ring_down(i).start()

    def right(h):
        return send(cots_z.at[z - h], cots_z.at[z - h], cz_s.at[h], cz_r.at[h], at(zz=z + 1))

    def left(h):
        return send(cots_z.at[z + h], cots_z.at[z + h], cz_s.at[3 + h], cz_r.at[3 + h], at(zz=z - 1))

    def line_wait(h):
        @pl.when(z >= h)
        def _():
            pltpu.make_async_copy(cots_z.at[0], cots_z.at[0], cz_r.at[h - 1]).wait()

        @pl.when(z < ZS - h)
        def _():
            pltpu.make_async_copy(cots_z.at[0], cots_z.at[0], cz_r.at[2 + h]).wait()

        if h < 3:

            @pl.when((z >= h) & (z < ZS - 1))
            def _():
                right(h).start()

            @pl.when((z < ZS - h) & (z > 0))
            def _():
                left(h).start()

    mine = pl.ds(pl.multiple_of(x * 32, 32), 32)
    h_copy = send(x_sum, h_in, h_s.at[0], h_r.at[0], other)
    totals = [
        send(total.at[mine], total.at[mine], x2_s.at[d - 1], x2_r.at[d - 1], x_off(d))
        for d in range(1, XS)
    ]

    x_parts = []
    for d in range(1, XS):
        rows = pl.ds(pl.multiple_of(lax.rem(x + d, XS) * 32, 32), 32)
        x_parts.append(send(decoded.at[rows], x_in.at[d - 1], x1_s.at[d - 1], x1_r.at[d - 1], x_off(d)))

    def share_codes():
        eye = lax.broadcasted_iota(jnp.int32, (128, 128), 0) == lax.broadcasted_iota(
            jnp.int32, (128, 128), 1
        )
        loads[3].wait()
        loads[4].wait()
        scales = jnp.exp2(exps[...].astype(F32))
        for b in range(4):
            cols = slice(b * 128, (b + 1) * 128)
            scale = column(scales[b : b + 1, :], eye)
            decoded[:, cols] = (codes[:, cols].astype(F32) * scale).astype(BF16)
        for copy in x_parts:
            copy.start()

    def gather_x():
        for copy in x_parts:
            copy.wait_recv()
        x_sum[...] = (
            decoded[mine, :].astype(F32) + x_in[0].astype(F32) + x_in[1].astype(F32) + x_in[2].astype(F32)
        )

        @pl.when(zh == 0)
        def _():
            pl.semaphore_wait(met, 1)

        h_copy.start()

    def spread_total():
        h_copy.wait_recv()
        total[mine, :] = x_sum[...] + h_in[...]
        for copy in totals:
            copy.start()

    total_copy = pltpu.make_async_copy(total, total_hbm, out_sem.at[0])

    def write_total():
        for copy in totals:
            copy.wait_recv()
        total_copy.start()

    push_z(0)

    @pl.when(core == 0)
    def _():
        push_y(0, (4, 3, 5))
        ring_wait(0)
        ring_go(1)
        push_y(0, (2, 6, 1, 7))
        share_codes()
        sent_z(0)
        push_z(1)
        push_y(1, (4, 3, 5))
        ring_wait(1)
        ring_go(2)
        push_y(1, (2, 6, 1, 7))
        gather_x()
        sent_z(1)
        push_z(2)
        push_y(2, (4, 3, 5))
        ring_wait(2)
        ring_go(3)
        push_y(2, (2, 6, 1, 7))
        sent_z(2)
        push_z(3)
        push_y(3, (4, 3, 5))
        across_1().wait_recv()
        ring_wait(3)
        multiply_y(0)
        push_y(3, (2, 6, 1, 7))
        pass_y(0)
        sent_z(3)
        push_z(4)
        multiply_y(1)
        pass_y(1)
        spread_total()
        multiply_y(2)
        pass_y(2)
        write_total()
        multiply_y(3)
        @pl.when(z > 0)
        def _():
            part[3] = part[3] + inbox(z)

        @pl.when(z < ZS - 1)
        def _():
            part[3] = part[3] + inbox(z + 4)

        result = pltpu.make_async_copy(part.at[3], summed_hbm, out_sem.at[1])
        result.start()
        result.wait()
        sent_y(0)
        sent_y(1)
        sent_y(2)
        sent_y(3)
        sent_z(4)

    @pl.when(core == 1)
    def _():
        line_wait(1)
        push_y(0)
        share_codes()
        sent_z(0)
        push_z(1)
        push_y(1, (4, 3, 5))
        line_wait(2)
        push_y(1, (2, 6, 1, 7))
        gather_x()
        sent_z(1)
        push_z(2)
        line_wait(3)
        across_0().wait_recv()
        multiply_z(0)
        chain(0)
        sent_z(2)
        push_z(3)
        push_y(2)
        multiply_z(1)
        chain(1)
        sent_z(3)
        push_z(4)
        push_y(3)
        multiply_z(2)
        chain(2)
        spread_total()
        multiply_z(3)
        chain(3)
        write_total()
        multiply_z(4)
        results = []
        for h in range(2):
            add_up(3, h, 7)
            add_down(3, h, 7)
            cols = slice(256 * h, 256 * h + 256)
            results.append(
                pltpu.make_async_copy(part.at[7, :, cols], summed_hbm.at[:, cols], out_sem.at[1 + h])
            )
            results[h].start()
        for result in results:
            result.wait()
        sent_y(0)
        sent_y(1)
        sent_y(2)
        sent_y(3)
        sent_z(4)

    total_copy.wait()
    for copy in first + x_parts + [h_copy] + totals:
        copy.wait_send()
    @pl.when(z < ZS - 1)
    def _():
        first_right().wait_send()

    @pl.when(z > 0)
    def _():
        first_left().wait_send()

    @pl.when(core == 0)
    def _():
        across_0().wait_send()
        for g in range(5):
            for i in groups[g]:
                own_z(g, i).wait_send()
        for i in range(1, 4):
            ring_up(i).wait_send()
            ring_down(i).wait_send()
        for k in range(3):
            z_copy(k).wait_send()

    @pl.when(core == 1)
    def _():
        across_1().wait_send()
        for k in range(4):
            own_y(k).wait_send()
        for h in (1, 2):

            @pl.when((z >= h) & (z < ZS - 1))
            def _():
                right(h).wait_send()

            @pl.when((z < ZS - h) & (z > 0))
            def _():
                left(h).wait_send()

        up_copy(0, 0).wait_send()
        down_copy(0, 1).wait_send()
        for s in range(1, 4):
            for h in range(2):
                up_copy(s, h).wait_send()
                down_copy(s, h).wait_send()


def finish(
    summed_hbm, total_hbm, weight_hbm, gain_hbm, global_hbm, momentum_hbm,
    local_out, gain_out, global_out, momentum_out,
    summed, total, weight, gain, outer, mom, local, gain_new, in_sem, out_sem,
):
    sources = (total_hbm, momentum_hbm, global_hbm, summed_hbm, weight_hbm.at[0], gain_hbm)
    loads = [
        pltpu.make_async_copy(src, dst, in_sem.at[i])
        for i, (src, dst) in enumerate(zip(sources, (total, mom, outer, summed, weight, gain)))
    ]
    for load in loads:
        load.start()
    for load in loads[:3]:
        load.wait()
    average = total[...] / 8.0
    mom[...] = 0.9 * mom[...] + average
    outer[...] = outer[...] - 0.7 * (average + 0.9 * mom[...])
    stores = [
        pltpu.make_async_copy(mom, momentum_out, out_sem.at[0]),
        pltpu.make_async_copy(outer, global_out, out_sem.at[1]),
    ]
    stores[0].start()
    stores[1].start()
    for load in loads[3:]:
        load.wait()
    eye = lax.broadcasted_iota(jnp.int32, (128, 128), 0) == lax.broadcasted_iota(
        jnp.int32, (128, 128), 1
    )
    root = math.sqrt(8192)
    held = weight[...].astype(F32)
    weight_grad = column(gain[...], eye) * summed[...] / root
    local[...] = 0.5 * (held - 0.2 * weight_grad) + 0.5 * outer[...]
    stores.append(pltpu.make_async_copy(local, local_out.at[0], out_sem.at[2]))
    stores[2].start()
    gain_grad = jnp.sum(held * summed[...], axis=1, keepdims=True) / root
    gain_row = jnp.sum(jnp.where(eye, gain_grad, 0.0), axis=0, keepdims=True)
    gain_new[...] = gain[...] - 0.005 * gain_row
    stores.append(pltpu.make_async_copy(gain_new, gain_out, out_sem.at[3]))
    stores[3].start()
    for store in stores:
        store.wait()


def shards(
    activations, cotangent, local_weight, norm_gain, global_weight, momentum, codes, exponents
):
    rows, width = global_weight.shape
    anywhere = pl.BlockSpec(memory_space=pl.ANY)
    sem = pltpu.SemaphoreType.DMA
    whole = jax.ShapeDtypeStruct((rows, width), F32)
    summed, total = pl.pallas_call(
        kernel,
        out_shape=(whole, whole),
        in_specs=[anywhere] * 4,
        out_specs=(anywhere,) * 2,
        scratch_shapes=[
            pltpu.VMEM((128, 8192), BF16),
            pltpu.VMEM((128, 512), BF16),
            pltpu.VMEM((32, 128, 128), BF16),
            pltpu.VMEM((32, 128, 128), BF16),
            pltpu.VMEM((4, 16, 128, 128), BF16),
            pltpu.VMEM((8, 8, 128, 128), BF16),
            pltpu.VMEM((8, 2, 128, 512), BF16),
            pltpu.VMEM((4, 2, 128, 512), BF16),
            pltpu.VMEM((128, 512), BF16),
            pltpu.VMEM((4, 128), jnp.int32),
            pltpu.VMEM((8, 128, 512), F32),
            pltpu.VMEM((7, 128, 512), F32),
            pltpu.VMEM((4, 128, 512), F32),
            pltpu.VMEM((4, 128, 512), F32),
            pltpu.VMEM((128, 512), BF16),
            pltpu.VMEM((3, 32, 512), BF16),
            pltpu.VMEM((32, 512), F32),
            pltpu.VMEM((32, 512), F32),
            pltpu.VMEM((128, 512), F32),
            sem((5,)),
            sem((3,)),
            sem((8,)),
            sem((9,)),
            sem((6,)),
            sem((7,)),
            sem((4,)),
            sem((4,)),
            sem((5,)),
            sem((5,)),
            sem((9,)),
            sem((3,)),
            sem((7,)),
            sem((4, 2)),
            sem((4, 2)),
            sem((4, 2)),
            sem((4, 2)),
            sem((3,)),
            sem((3,)),
            sem((1,)),
            sem((1,)),
            sem((3,)),
            sem((3,)),
            pltpu.SemaphoreType.REGULAR,
        ],
        compiler_params=pltpu.CompilerParams(
            collective_id=0, has_side_effects=True, vmem_limit_bytes=60 << 20
        ),
        name="exchange",
    )(activations, cotangent, codes, jnp.transpose(exponents[0]))
    return pl.pallas_call(
        finish,
        out_shape=(
            jax.ShapeDtypeStruct((1, rows, width), F32),
            jax.ShapeDtypeStruct((1, rows), F32),
            whole,
            whole,
        ),
        in_specs=[anywhere] * 6,
        out_specs=(anywhere,) * 4,
        scratch_shapes=[
            pltpu.VMEM((128, 512), F32),
            pltpu.VMEM((128, 512), F32),
            pltpu.VMEM((128, 512), BF16),
            pltpu.VMEM((1, 128), F32),
            pltpu.VMEM((128, 512), F32),
            pltpu.VMEM((128, 512), F32),
            pltpu.VMEM((128, 512), F32),
            pltpu.VMEM((1, 128), F32),
            sem((6,)),
            sem((4,)),
        ],
        compiler_params=pltpu.CompilerParams(vmem_limit_bytes=60 << 20),
        name="finish",
    )(summed, total, local_weight, norm_gain, global_weight, momentum)


def solution(mesh):
    placed = (
        P("rep", "fsdp", None),
        P("rep", "fsdp", None),
        P("rep", "fsdp", None),
        P("rep", "fsdp"),
        P("fsdp", None),
        P("fsdp", None),
        P("rep", "fsdp", None),
        P("rep", "fsdp", None),
    )
    return jax.shard_map(
        shards,
        mesh=mesh,
        in_specs=placed,
        out_specs=(P("rep", "fsdp", None), P("rep", "fsdp"), P("fsdp", None), P("fsdp", None)),
        check_vma=False,
    )
```
